32 devices in a mesh: gx: 4 (over y, x), gy: 4 (over z), gz: 2 (over core).
Axes of the slice: x: 2, y: 2, z: 4, core: 2. Of those that a mesh axis runs over, the one named last changes fastest.
Arguments:
- nodal_field: float32 [128, 512, 512], P('gx', 'gy', 'gz'), may hold values from -6 to 6
- spacing_x: float32 [128], replicated, may hold values from 0.5 to 2
- spacing_z: float32 [512], replicated, may hold values from 0.5 to 2
- operator_x: float32 [64, 16], P('gx'), may hold values from -1.5 to 1.5
- persist_x: float32 [64], P('gx'), may hold values from 0.6 to 1
- operator_z: float32 [256, 128], P('gz'), may hold values from -0.5 to 0.5
- persist_z: float32 [256], P('gz'), may hold values from 0.6 to 1
- receivers: int32 [16384, 1], P(('gx', 'gy', 'gz')), may hold values from 0 to 7; in each aligned block of 512 rows (0 to 511, 512 to 1023, ...) at most 128 rows name the same one
Outputs:
- detail_x: float32 [64, 512, 512], P('gx', 'gy', 'gz')
- detail_z: float32 [64, 512, 256], P('gx', 'gy', 'gz')
- received: float32 [32, 8, 128, 2, 4, 128], P(('gx', 'gy', 'gz'))
The draws below stay inside these ranges and needn't reach their ends.
Inputs may be any that keep to these rules, and one draw needn't show every extreme that they name: `receivers`: each row names the receiving device of one kept block among the 8 devices with the same gx index, in (gy, gz) row-major order; of the 512 blocks of one device at most 128 name the same receiver, and that bound is reached.
All inputs are finite; a program needn't handle non-finite values.
Results may differ from the reference program's by a relative error of at most 0.00008.
Values sent between devices are 32-bit elements; how exact they have to be, the bound alone decides.
A program may use at most 64 MiB of HBM per device.

```python
import math
import jax
import jax.numpy as jnp
import numpy as np
from jax import lax

CY = 128
LINES = 4
HX = 16
HZ = 128
NB = 512
MOST = 128
NX = 128
NY = 512
NZ = 512
N_GX = 4
N_GY = 4
N_GZ = 2
DEVICES = 32


def block_scale(key, dims, shards, least, largest):
    def one(position, blocks):
        heights = jax.random.uniform(jax.random.fold_in(jax.random.fold_in(key, 6), position), (blocks,), jnp.float32, least / len(shards), largest / len(shards))
        return jnp.repeat(jnp.exp(heights), dims[position] // blocks).reshape((-1,) + (1,) * (len(dims) - position - 1))

    gain = one(*shards[0])
    for cut in shards[1:]:
        gain = gain * one(*cut)
    return gain


def deal_out(key, own, number, rows, amount, top, reach, slope):
    order = jax.random.permutation(key, amount)
    heavy_load, common = portions_of(amount, rows * top, reach, slope, True), portions_of(amount, rows * top, reach, slope, False)
    places = jnp.arange(amount)

    def named(tallies, offset_by):
        used = int((tallies > 0).sum())
        fixed = max(1, used // 4)
        moved = fixed + (places - fixed + offset_by * (used - fixed)) % max(1, amount - fixed)
        return jnp.zeros((amount,), jnp.int32).at[order[jnp.where(places < fixed, places, moved)]].set(jnp.asarray(tallies, jnp.int32))

    tallies = jnp.where(number % 4 == 0, named(heavy_load, number // 4), named(common, number - number // 4 - 1))
    mixed = jax.random.permutation(jax.random.fold_in(own, 3), amount)
    source_of, taker = mixed[0:amount // 2 * 2:2], mixed[1:amount // 2 * 2:2]
    room = jnp.minimum(tallies[source_of] - 1, reach - tallies[taker]) // 2
    room = jnp.where((source_of == order[0]) | (taker == order[0]) | (tallies[taker] == 0), 0, jnp.maximum(room, 0))
    moved = jax.random.randint(jax.random.fold_in(own, 4), (amount // 2,), 0, 1 << 20) % (room + 1)
    tallies = tallies.at[source_of].add(-moved).at[taker].add(moved)
    members = jnp.searchsorted(jnp.cumsum(tallies), jnp.arange(rows * top), side="right").astype(jnp.int32)
    listing = members.reshape(top, rows).T
    listing = listing[jax.random.permutation(jax.random.fold_in(own, 1), rows)]
    offset_by = jax.random.randint(jax.random.fold_in(own, 2), (rows, 1), 0, top)
    return jnp.take_along_axis(listing, (jnp.arange(top)[None, :] + offset_by) % top, axis=1)


def portions_of(number_of, total, most, lean, full):
    portions = [(1 << 20) // math.isqrt(standing ** lean) + 1 for standing in range(1, number_of + 1)]
    largest = most if full else min(most, max(-(-total // number_of), total * portions[0] // sum(portions)))
    least = 1 if total - largest >= number_of - 1 else 0
    holding, rest = [largest] + [least] * (number_of - 1), total - largest - least * (number_of - 1)
    while rest > 0:
        free = [i for i in range(1, number_of) if holding[i] < largest] or [i for i in range(1, number_of) if holding[i] < most]
        whole, left = sum([portions[i] for i in free]), rest
        for i in free:
            more = min(most - holding[i], max(1, left * portions[i] // whole), rest)
            holding[i] = holding[i] + more
            rest = rest - more
    return np.array(holding)


def centred(own_key, dims, scale, limit, cuts=(), kind=jnp.bfloat16):
    result = jax.random.normal(own_key, dims, jnp.float32) * scale
    if len(cuts) > 0:
        result = block_scale(own_key, dims, cuts, -0.22, 0.18) * result
    return jnp.clip(result, min=-limit, max=limit).astype(kind)


def setup_inputs(seed: int = 0) -> dict:
    keys = jax.random.split(jax.random.key(seed), 9)
    nodal_field = centred(keys[0], (NX, NY, NZ), 1.0, 6.0, ((0, 4), (1, 4), (2, 2)), jnp.float32)
    spacing_x = jnp.clip(jnp.exp(jax.random.uniform(keys[1], (NX,), jnp.float32, math.log(0.5), math.log(2.0))), 0.5, 2.0)
    spacing_z = jnp.clip(jnp.exp(jax.random.uniform(keys[2], (NZ,), jnp.float32, math.log(0.5), math.log(2.0))), 0.5, 2.0)
    operator_x = centred(keys[3], (NX // 2, HX), HX ** -0.5, 1.5, ((0, 4),), jnp.float32)
    persist_x = jnp.clip(0.6 + 0.39999998 * jax.random.uniform(keys[4], (NX // 2,), jnp.float32) ** block_scale(keys[4], (NX // 2,), ((0, 4),), -0.2, 0.2), 0.6, 1.0)
    operator_z = centred(keys[5], (NZ // 2, HZ), HZ ** -0.5, 0.5, ((0, 2),), jnp.float32)
    persist_z = jnp.clip(0.6 + 0.39999998 * jax.random.uniform(keys[6], (NZ // 2,), jnp.float32) ** block_scale(keys[6], (NZ // 2,), ((0, 2),), -0.2, 0.2), 0.6, 1.0)
    receivers_keys = jax.random.split(jax.random.fold_in(keys[7], 1), (DEVICES * NB) // NB)
    receivers_turns = jax.random.permutation(jax.random.fold_in(keys[7], 3), (DEVICES * NB) // NB)
    receivers = jax.vmap(lambda own, number: deal_out(jax.random.fold_in(keys[7], 2), own, number, NB, N_GY * N_GZ, 1, MOST, 2))(receivers_keys, receivers_turns).reshape((DEVICES * NB, 1))
    return dict(nodal_field=nodal_field, spacing_x=spacing_x, spacing_z=spacing_z, operator_x=operator_x, persist_x=persist_x, operator_z=operator_z, persist_z=persist_z, receivers=receivers)


def refine(nodes, spacing, row_blocks, gain_list, parts):
    length = nodes.shape[0]
    coarse_count = length // 2
    block_len = coarse_count // parts
    space_even = spacing[0::2]
    space_odd = spacing[1::2]
    span_sum = space_even + space_odd
    weight_a = (space_odd / span_sum)[:, None, None]
    weight_b = (space_even / span_sum)[:, None, None]
    even_nodes = nodes[0::2]
    odd_nodes = nodes[1::2]
    right_nodes = jnp.concatenate([even_nodes[1:], jnp.zeros_like(even_nodes[:1])], 0)
    detail = odd_nodes - weight_a * even_nodes - weight_b * right_nodes
    near_terms = (0.5 * space_even)[:, None, None] * detail
    far_terms = (0.5 * space_odd)[:, None, None] * detail
    load_terms = near_terms + jnp.concatenate([jnp.zeros_like(far_terms[:1]), far_terms[:-1]], 0)
    line_count = load_terms.shape[1] * load_terms.shape[2]
    grouped = load_terms.reshape(parts, block_len, line_count)
    operators = row_blocks.reshape(parts, block_len, block_len)
    local_part = jnp.einsum("pij,pjm->pim", operators, grouped, precision=lax.Precision.HIGHEST)
    gain_blocks = gain_list.reshape(parts, block_len, 1)
    carried = jnp.zeros_like(local_part[0, 0])
    pieces = []
    for member in range(parts):
        solved = local_part[member] + gain_blocks[member] * carried[None, :]
        pieces.append(solved)
        carried = solved[-1]
    solved_all = jnp.stack(pieces, 0).reshape(load_terms.shape)
    return detail, even_nodes + solved_all


def reference(nodal_field, spacing_x, spacing_z, operator_x, persist_x, operator_z, persist_z, receivers):
    detail_x, coarse_x = refine(nodal_field, spacing_x, operator_x, persist_x, N_GX)
    moved_detail, moved_coarse = refine(jnp.moveaxis(coarse_x, 2, 0), spacing_z, operator_z, persist_z, N_GZ)
    detail_z = jnp.moveaxis(moved_detail, 0, 2)
    coarse_z = jnp.moveaxis(moved_coarse, 0, 2)
    group_size = N_GY * N_GZ
    device_count = N_GX * group_size

    def bricks(array):
        shaped = array.reshape(N_GX, HX, N_GY, CY, N_GZ, HZ).transpose(0, 2, 4, 1, 3, 5)
        return shaped.reshape(device_count, NB, LINES, HZ)

    tile_rows = jnp.stack([bricks(coarse_z), bricks(detail_z)], 2)
    targets = receivers.reshape(device_count, NB).astype(jnp.int32)
    positions = jnp.arange(NB, dtype=jnp.int32)
    earlier = (targets[:, None, :] == targets[:, :, None]) & (positions[None, None, :] < positions[None, :, None])
    slots = jnp.sum(earlier.astype(jnp.int32), axis=2).astype(jnp.int32)
    senders = jnp.broadcast_to(jnp.arange(device_count, dtype=jnp.int32)[:, None], targets.shape)
    outgoing = jnp.zeros((device_count, group_size * MOST, 2, LINES, HZ), jnp.float32)
    outgoing = outgoing.at[senders, targets * MOST + slots].set(tile_rows)
    arranged = outgoing.reshape(N_GX, group_size, group_size, MOST, 2, LINES, HZ).transpose(0, 2, 1, 3, 4, 5, 6)
    return detail_x, detail_z, arranged.reshape(device_count, group_size, MOST, 2, LINES, HZ)
```

```python
import functools

import jax
import jax.numpy as jnp
from jax import lax
from jax.experimental import pallas as pl
from jax.experimental.pallas import tpu as pltpu
from jax.sharding import PartitionSpec as P

LINES = 4
MESH = pl.DeviceIdType.MESH
HIGHEST = lax.Precision.HIGHEST
LIMIT = 40 * 1024 * 1024


def coefficients(spacing):
    pairs = spacing.reshape(-1, 2)
    even, odd = pairs[:, 0], pairs[:, 1]
    total = even + odd
    a, b = odd / total, even / total

    def before(row):
        return jnp.concatenate([jnp.zeros_like(row[:1]), row[:-1]])

    zero = jnp.zeros_like(a)
    return jnp.stack(
        [a, b, 0.5 * even, before(0.5 * odd), before(a), before(b), zero, zero]
    )


def exchange_first(count, nodes, coefs, factor, gain, out, left, right, send, tails, sems):
    me = lax.axis_index("gx")
    half = nodes.shape[0] // 2
    lines = nodes.shape[1]
    total = count * half
    send_sem, recv_sem = sems
    barrier = pltpu.get_barrier_semaphore()
    for d in range(1, count):
        pl.semaphore_signal(
            barrier, inc=1, device_id={"gx": lax.rem(me + d, count)}, device_id_type=MESH
        )

    def coef(row, k):
        return coefs[row * total + me * half + k]

    last = half - 1
    send[1, pl.ds(0, lines), :] = nodes[2 * last + 1] - coef(0, last) * nodes[2 * last]
    pl.semaphore_wait(barrier, count - 1)

    to_right = pltpu.make_async_remote_copy(
        src_ref=send.at[1, pl.ds(0, lines)], dst_ref=left, send_sem=send_sem.at[0], recv_sem=recv_sem.at[0],
        device_id={"gx": lax.rem(me + 1, count)}, device_id_type=MESH,
    )
    to_left = pltpu.make_async_remote_copy(
        src_ref=nodes.at[0], dst_ref=right, send_sem=send_sem.at[1], recv_sem=recv_sem.at[1],
        device_id={"gx": lax.rem(me + count - 1, count)}, device_id_type=MESH,
    )

    @pl.when(me < count - 1)
    def _():
        to_right.start()

    @pl.when(me > 0)
    def _():
        to_left.start()

    weights = []
    for k in range(half):
        weight = factor[last, k] * coef(2, k)
        if k < last:
            weight = weight + factor[last, k + 1] * coef(3, k + 1)
        weights.append(weight)
    edge = factor[last, 0] * coef(3, 0)

    def chunk(i, carry):
        rows = pl.ds(pl.multiple_of(i * 8, 8), 8)
        even = nodes[0, rows, :]
        value = (-edge * coef(5, 0)) * even
        for k in range(half):
            detail = nodes[2 * k + 1, rows, :] - coef(0, k) * even
            if k < last:
                even = nodes[2 * k + 2, rows, :]
                detail = detail - coef(1, k) * even
            value = value + weights[k] * detail
        send[0, rows, :] = value
        return carry

    lax.fori_loop(0, lines // 8, chunk, 0)

    @pl.when(me == 0)
    def _():
        left[...] = jnp.zeros_like(left)

    @pl.when(me == count - 1)
    def _():
        right[...] = jnp.zeros_like(right)

    @pl.when(me > 0)
    def _():
        to_right.wait_recv()

    @pl.when(me < count - 1)
    def _():
        to_left.wait_recv()

    end = -(factor[last, last] * coef(2, last)) * coef(1, last)
    own = send.at[0]
    own[pl.ds(0, lines), :] = own[pl.ds(0, lines), :] + edge * left[...] + end * right[...]
    own[pl.ds(lines, 8), :] = jnp.full((8, own.shape[1]), gain[last], jnp.float32)

    copies = []
    for d in range(1, count):
        copies.append(
            pltpu.make_async_remote_copy(
                src_ref=tails.at[0], dst_ref=tails.at[d],
                send_sem=send_sem.at[1 + d], recv_sem=recv_sem.at[1 + d],
                device_id={"gx": lax.rem(me + d, count)}, device_id_type=MESH,
            )
        )
    tails[0] = own[...]
    for d in range(1, count):

        @pl.when(me + d < count)
        def _(d=d):
            copies[d - 1].start()

    out[0] = left[...]
    out[1] = right[...]
    out[2] = jnp.zeros_like(left)
    for d in range(count - 1, 0, -1):

        @pl.when(me >= d)
        def _(d=d):
            copies[d - 1].wait_recv()
            out[2] = (
                tails[d, pl.ds(0, lines), :]
                + jnp.max(tails[d, pl.ds(lines, 8), :], axis=0, keepdims=True) * out[2]
            )

    @pl.when(me < count - 1)
    def _():
        to_right.wait_send()

    @pl.when(me > 0)
    def _():
        to_left.wait_send()

    for d in range(1, count):

        @pl.when(me + d < count)
        def _(d=d):
            copies[d - 1].wait_send()


def loads(coefz):
    width = coefz.shape[1]
    row = lax.broadcasted_iota(jnp.int32, (2 * width, width), 0)
    twice = 2 * lax.broadcasted_iota(jnp.int32, (2 * width, width), 1)
    a, b, half_even, half_odd, a_before, b_before = [coefz[k : k + 1, :] for k in range(6)]
    zero = jnp.zeros((2 * width, width), jnp.float32)
    detail = jnp.where(row == twice, -a, zero)
    detail = jnp.where(row == twice + 1, 1.0, detail)
    detail = jnp.where(row == twice + 2, -b, detail)
    earlier = jnp.where(row == twice - 2, -a_before, zero)
    earlier = jnp.where(row == twice - 1, 1.0, earlier)
    earlier = jnp.where(row == twice, -b_before, earlier)
    return detail, half_even * detail + half_odd * earlier, row == twice


def first_kernel(
    nodes, planes, coefs, factor, gain, coefz, factor_z, gain_z, detail, coarse, payload,
    weights, *, count,
):
    me = lax.axis_index("gx")
    half = detail.shape[0]
    total = count * half

    def coef(row, k):
        return coefs[row * total + me * half + k]

    width = factor_z.shape[0]

    @pl.when(pl.program_id(0) == 0)
    def _():
        load = loads(coefz)[1]
        tail = lax.dot_general(
            factor_z[pl.ds(width - 8, 8), :], load, (((1,), (1,)), ((), ())), precision=HIGHEST
        )
        lane = lax.broadcasted_iota(jnp.int32, (1, 2 * width), 1)
        a_last = coefz[0:1, width - 1 : width]
        weights[...] = jnp.zeros_like(weights)
        weights[0:1, :] = jnp.where(lane == 0, 1.0, 0.0)
        weights[1:2, :] = jnp.where(
            lane == 2 * width - 2, -a_last, jnp.where(lane == 2 * width - 1, 1.0, 0.0)
        )
        weights[2:3, :] = tail[7:8, :]

    for i in range(nodes.shape[1] // 8):
        rows = pl.ds(i * 8, 8)
        even = [nodes[2 * k, rows, :] for k in range(half)]
        before = planes[0, rows, :] - coef(5, 0) * even[0]
        load = []
        for k in range(half):
            after = even[k + 1] if k + 1 < half else planes[1, rows, :]
            value = nodes[2 * k + 1, rows, :] - coef(0, k) * even[k] - coef(1, k) * after
            detail[k, rows, :] = value
            load.append(coef(2, k) * value + coef(3, k) * before)
            before = value
        for k in range(half):
            value = nodes[2 * k, rows, :] + gain[k] * planes[2, rows, :]
            for j in range(half):
                value = value + factor[k, j] * load[j]
            coarse[k, rows, :] = value

    lines = coarse[...].reshape(half * coarse.shape[1], coarse.shape[2])
    sent = lax.dot_general(
        weights[...], lines, (((1,), (1,)), ((), ())), precision=HIGHEST
    )
    kind = lax.broadcasted_iota(jnp.int32, sent.shape, 0)
    end_gain = gain_z[0:1, width - 1 : width]
    end_first = factor_z[width - 1 : width, 0:1] * coefz[3:4, 0:1]
    end_last = -(
        factor_z[width - 1 : width, width - 1 : width]
        * coefz[2:3, width - 1 : width]
        * coefz[1:2, width - 1 : width]
    )
    sent = jnp.where(kind == 3, end_gain, sent)
    sent = jnp.where(kind == 4, end_first, sent)
    sent = jnp.where(kind == 5, end_last, sent)
    payload[0] = sent


def third_kernel(
    placed, coarse, gathered, coefz, factor_z, gain_z, detail, outgoing, matrix, update, tiles,
    *, count, chunks,
):
    me = lax.axis_index("gz")
    step = pl.program_id(0)
    width = factor_z.shape[0]

    @pl.when(step == 0)
    def _():
        outgoing[...] = jnp.zeros_like(outgoing)
        detail_of, load_of, is_even = loads(coefz)
        solved = lax.dot_general(
            load_of, factor_z[...], (((1,), (1,)), ((), ())), precision=HIGHEST
        )
        matrix[:, 0:width] = jnp.where(is_even, 1.0, 0.0) + solved
        matrix[:, width:] = detail_of
        turned = factor_z[...].T
        b_last = coefz[1:2, width - 1 : width]
        lane = lax.broadcasted_iota(jnp.int32, (1, width), 1)
        update[...] = jnp.zeros_like(update)
        update[0:1, 0:width] = -turned[width - 1 : width, :] * (
            coefz[2:3, width - 1 : width] * b_last
        )
        update[0:1, width:] = jnp.where(lane == width - 1, -b_last, 0.0)
        update[1:2, 0:width] = turned[0:1, :] * coefz[3:4, 0:1]
        update[2:3, 0:width] = gain_z[...]

    def heard(p, row):
        return gathered[p, 0, row : row + 1, :]

    empty = jnp.zeros_like(heard(0, 0))
    right, left, carry = empty, empty, empty
    for p in range(count):
        right = jnp.where(me + 1 == p, heard(p, 0), right)
        left = jnp.where(me - 1 == p, heard(p, 1), left)
        if p < count - 1:
            tail = heard(p, 2) + heard(p, 5) * heard(p + 1, 0) + heard(p, 3) * carry
            if p > 0:
                tail = tail + heard(p, 4) * heard(p - 1, 1)
            carry = jnp.where(p < me, tail, carry)
    kind = lax.broadcasted_iota(jnp.int32, (8, empty.shape[1]), 0)
    edges = jnp.where(kind == 0, right, jnp.where(kind == 1, left, jnp.where(kind == 2, carry, 0.0)))

    rows = coarse.shape[0] * coarse.shape[1]
    lines = coarse[...].reshape(rows, coarse.shape[2])
    result = jnp.dot(lines, matrix[...], precision=HIGHEST) + lax.dot_general(
        edges, update[...], (((0,), (0,)), ((), ())), precision=HIGHEST
    )
    upper = result[:, :width].reshape(rows // 8, 8, width)
    lower = result[:, width:].reshape(rows // 8, 8, width)
    detail[...] = result[:, width:].reshape(detail.shape)
    top = lax.broadcasted_iota(jnp.int32, upper.shape, 1) < LINES
    tiles[0] = jnp.where(top, upper, pltpu.roll(lower, LINES, 1))
    tiles[1] = jnp.where(top, pltpu.roll(upper, LINES, 1), lower)
    eights = coarse.shape[1] // 8

    def scatter(x, carry):
        for j in range(eights):
            for half in range(2):
                block = x * (2 * eights * chunks) + step * (2 * eights) + 2 * j + half
                outgoing[placed[block]] = tiles[half, x * eights + j]
        return carry

    lax.fori_loop(0, coarse.shape[0], scatter, 0)


def deliver_kernel(n_gy, n_gz, outgoing, received, send_sem, recv_sem, own_sem):
    gy, gz = lax.axis_index("gy"), lax.axis_index("gz")
    me = gy * n_gz + gz
    shifts = [
        (dy, dz) for dy in range(n_gy) for dz in range(n_gz) if dy + dz > 0
    ]
    shifts.sort(key=lambda shift: -min(shift[0], n_gy - shift[0]))
    barrier = pltpu.get_barrier_semaphore()
    targets = []
    for dy, dz in shifts:
        there = (lax.rem(gy + dy, n_gy), lax.rem(gz + dz, n_gz))
        targets.append(there)
        pl.semaphore_signal(
            barrier, inc=1, device_id={"gy": there[0], "gz": there[1]}, device_id_type=MESH
        )
    own = pltpu.make_async_copy(outgoing.at[me], received.at[me], own_sem)
    own.start()
    pl.semaphore_wait(barrier, len(shifts))
    copies = []
    for k, there in enumerate(targets):
        copy = pltpu.make_async_remote_copy(
            src_ref=outgoing.at[there[0] * n_gz + there[1]],
            dst_ref=received.at[me],
            send_sem=send_sem.at[k],
            recv_sem=recv_sem.at[k],
            device_id={"gy": there[0], "gz": there[1]},
            device_id_type=MESH,
        )
        copy.start()
        copies.append(copy)
    own.wait()
    for copy in copies:
        copy.wait()


def local(sizes, nodes, spacing_x, spacing_z, factor_x, gain_x, factor_z, gain_z, receivers):
    n_gx, n_gy, n_gz = sizes
    length, lines, depth = nodes.shape
    half, width = length // 2, depth // 2
    coefs = coefficients(spacing_x).reshape(-1)
    coefz = lax.dynamic_slice_in_dim(
        coefficients(spacing_z), lax.axis_index("gz") * width, width, axis=1
    )
    gain_row = gain_z.reshape(1, width)
    vmem = pl.BlockSpec(memory_space=pltpu.VMEM)
    smem = pl.BlockSpec(memory_space=pltpu.SMEM)
    hbm = pl.BlockSpec(memory_space=pl.ANY)

    def exchange(nodes, coefs, factor, gain, out, left, right, send, tails, s_sem, r_sem):
        exchange_first(
            n_gx, nodes, coefs, factor, gain, out, left, right, send, tails, (s_sem, r_sem)
        )

    planes = pl.pallas_call(
        exchange,
        out_shape=jax.ShapeDtypeStruct((3, lines, depth), jnp.float32),
        in_specs=[vmem, smem, smem, smem],
        out_specs=vmem,
        scratch_shapes=[
            pltpu.VMEM((lines, depth), jnp.float32),
            pltpu.VMEM((lines, depth), jnp.float32),
            pltpu.VMEM((2, lines + 8, depth), jnp.float32),
            pltpu.VMEM((n_gx, lines + 8, depth), jnp.float32),
            pltpu.SemaphoreType.DMA((n_gx + 1,)),
            pltpu.SemaphoreType.DMA((n_gx + 1,)),
        ],
        compiler_params=pltpu.CompilerParams(
            collective_id=0, has_side_effects=True, vmem_limit_bytes=LIMIT
        ),
        name="exchange_first",
    )(nodes, coefs, factor_x, gain_x)

    chunks = 4
    rows = lines // chunks
    params = pltpu.CompilerParams(
        dimension_semantics=("arbitrary",), vmem_limit_bytes=LIMIT
    )
    detail_x, coarse_x, payload = pl.pallas_call(
        functools.partial(first_kernel, count=n_gx),
        grid=(chunks,),
        in_specs=[
            pl.BlockSpec((length, rows, depth), lambda i: (0, i, 0)),
            pl.BlockSpec((3, rows, depth), lambda i: (0, i, 0)),
            smem, smem, smem,
            pl.BlockSpec((8, width), lambda i: (0, 0)),
            pl.BlockSpec((width, width), lambda i: (0, 0)),
            pl.BlockSpec((1, width), lambda i: (0, 0)),
        ],
        out_specs=[
            pl.BlockSpec((half, rows, depth), lambda i: (0, i, 0)),
            pl.BlockSpec((half, rows, depth), lambda i: (0, i, 0)),
            pl.BlockSpec((1, 8, half * rows), lambda i: (i, 0, 0)),
        ],
        out_shape=[
            jax.ShapeDtypeStruct((half, lines, depth), jnp.float32),
            jax.ShapeDtypeStruct((half, lines, depth), jnp.float32),
            jax.ShapeDtypeStruct((chunks, 8, half * rows), jnp.float32),
        ],
        scratch_shapes=[pltpu.VMEM((8, depth), jnp.float32)],
        compiler_params=params,
        name="pass_first",
    )(nodes, planes, coefs, factor_x, gain_x, coefz, factor_z, gain_row)

    gathered = lax.all_gather(payload, "gz")

    blocks = half * lines // LINES
    group = n_gy * n_gz
    capacity = max(2, blocks // group * 2)
    targets = receivers[:, 0]
    positions = jnp.arange(blocks, dtype=jnp.int32)
    earlier = (targets[None, :] == targets[:, None]) & (positions[None, :] < positions[:, None])
    placed = targets * capacity + jnp.sum(earlier.astype(jnp.int32), axis=1)

    detail_z, outgoing = pl.pallas_call(
        functools.partial(third_kernel, count=n_gz, chunks=chunks),
        grid=(chunks,),
        in_specs=[
            smem,
            pl.BlockSpec((half, rows, depth), lambda i: (0, i, 0)),
            pl.BlockSpec((n_gz, 1, 8, half * rows), lambda i: (0, i, 0, 0)),
            pl.BlockSpec((8, width), lambda i: (0, 0)),
            pl.BlockSpec((width, width), lambda i: (0, 0)),
            pl.BlockSpec((1, width), lambda i: (0, 0)),
        ],
        out_specs=[
            pl.BlockSpec((half, rows, width), lambda i: (0, i, 0)),
            pl.BlockSpec((group * capacity, 2 * LINES, width), lambda i: (0, 0, 0)),
        ],
        out_shape=[
            jax.ShapeDtypeStruct((half, lines, width), jnp.float32),
            jax.ShapeDtypeStruct((group * capacity, 2 * LINES, width), jnp.float32),
        ],
        scratch_shapes=[
            pltpu.VMEM((depth, depth), jnp.float32),
            pltpu.VMEM((8, depth), jnp.float32),
            pltpu.VMEM((2, half * rows // 8, 8, width), jnp.float32),
        ],
        compiler_params=params,
        name="pass_third",
    )(placed, coarse_x, gathered, coefz, factor_z, gain_row)

    outgoing = outgoing.reshape(group, capacity, 2 * LINES, width)
    received = pl.pallas_call(
        functools.partial(deliver_kernel, n_gy, n_gz),
        out_shape=jax.ShapeDtypeStruct(outgoing.shape, jnp.float32),
        in_specs=[hbm],
        out_specs=hbm,
        scratch_shapes=[
            pltpu.SemaphoreType.DMA((group - 1,)),
            pltpu.SemaphoreType.DMA((group - 1,)),
            pltpu.SemaphoreType.DMA,
        ],
        compiler_params=pltpu.CompilerParams(collective_id=1, has_side_effects=True),
        name="deliver",
    )(outgoing)
    return (
        detail_x,
        detail_z,
        received.reshape(1, group, capacity, 2, LINES, width),
    )


def solution(mesh):
    sizes = tuple(mesh.shape[axis] for axis in ("gx", "gy", "gz"))
    return jax.shard_map(
        functools.partial(local, sizes),
        mesh=mesh,
        in_specs=(
            P("gx", "gy", "gz"),
            P(),
            P(),
            P("gx", None),
            P("gx"),
            P("gz", None),
            P("gz"),
            P(("gx", "gy", "gz"), None),
        ),
        out_specs=(
            P("gx", "gy", "gz"),
            P("gx", "gy", "gz"),
            P(("gx", "gy", "gz"), None, None, None, None, None),
        ),
        check_vma=False,
    )
```

```python
import functools

import jax
import jax.numpy as jnp
from jax import lax
from jax.experimental import pallas as pl
from jax.experimental.pallas import tpu as pltpu
from jax.sharding import PartitionSpec as P

LINES = 4
MESH = pl.DeviceIdType.MESH
HIGHEST = lax.Precision.HIGHEST
LIMIT = 40 * 1024 * 1024


def coefficients(spacing):
    pairs = spacing.reshape(-1, 2)
    even, odd = pairs[:, 0], pairs[:, 1]
    total = even + odd
    a, b = odd / total, even / total

    def before(row):
        return jnp.concatenate([jnp.zeros_like(row[:1]), row[:-1]])

    zero = jnp.zeros_like(a)
    return jnp.stack(
        [a, b, 0.5 * even, before(0.5 * odd), before(a), before(b), zero, zero]
    )


def exchange_first(count, nodes, coefs, factor, gain, out, left, right, send, tails, sems):
    me = lax.axis_index("gx")
    half = nodes.shape[0] // 2
    lines = nodes.shape[1]
    total = count * half
    send_sem, recv_sem = sems
    barrier = pltpu.get_barrier_semaphore()
    for d in range(1, count):
        pl.semaphore_signal(
            barrier, inc=1, device_id={"gx": lax.rem(me + d, count)}, device_id_type=MESH
        )

    def coef(row, k):
        return coefs[row * total + me * half + k]

    last = half - 1
    send[1, pl.ds(0, lines), :] = nodes[2 * last + 1] - coef(0, last) * nodes[2 * last]
    pl.semaphore_wait(barrier, count - 1)

    to_right = pltpu.make_async_remote_copy(
        src_ref=send.at[1, pl.ds(0, lines)], dst_ref=left, send_sem=send_sem.at[0], recv_sem=recv_sem.at[0],
        device_id={"gx": lax.rem(me + 1, count)}, device_id_type=MESH,
    )
    to_left = pltpu.make_async_remote_copy(
        src_ref=nodes.at[0], dst_ref=right, send_sem=send_sem.at[1], recv_sem=recv_sem.at[1],
        device_id={"gx": lax.rem(me + count - 1, count)}, device_id_type=MESH,
    )

    @pl.when(me < count - 1)
    def _():
        to_right.start()

    @pl.when(me > 0)
    def _():
        to_left.start()

    weights = []
    for k in range(half):
        weight = factor[last, k] * coef(2, k)
        if k < last:
            weight = weight + factor[last, k + 1] * coef(3, k + 1)
        weights.append(weight)
    edge = factor[last, 0] * coef(3, 0)

    def chunk(i, carry):
        rows = pl.ds(pl.multiple_of(i * 8, 8), 8)
        even = nodes[0, rows, :]
        value = (-edge * coef(5, 0)) * even
        for k in range(half):
            detail = nodes[2 * k + 1, rows, :] - coef(0, k) * even
            if k < last:
                even = nodes[2 * k + 2, rows, :]
                detail = detail - coef(1, k) * even
            value = value + weights[k] * detail
        send[0, rows, :] = value
        return carry

    lax.fori_loop(0, lines // 8, chunk, 0)

    @pl.when(me == 0)
    def _():
        left[...] = jnp.zeros_like(left)

    @pl.when(me == count - 1)
    def _():
        right[...] = jnp.zeros_like(right)

    @pl.when(me > 0)
    def _():
        to_right.wait_recv()

    @pl.when(me < count - 1)
    def _():
        to_left.wait_recv()

    end = -(factor[last, last] * coef(2, last)) * coef(1, last)
    own = send.at[0]
    own[pl.ds(0, lines), :] = own[pl.ds(0, lines), :] + edge * left[...] + end * right[...]
    own[pl.ds(lines, 8), :] = jnp.full((8, own.shape[1]), gain[last], jnp.float32)

    copies = []
    for d in range(1, count):
        copies.append(
            pltpu.make_async_remote_copy(
                src_ref=tails.at[0], dst_ref=tails.at[d],
                send_sem=send_sem.at[1 + d], recv_sem=recv_sem.at[1 + d],
                device_id={"gx": lax.rem(me + d, count)}, device_id_type=MESH,
            )
        )
    tails[0] = own[...]
    for d in range(1, count):

        @pl.when(me + d < count)
        def _(d=d):
            copies[d - 1].start()

    out[0] = left[...]
    out[1] = right[...]
    out[2] = jnp.zeros_like(left)
    for d in range(count - 1, 0, -1):

        @pl.when(me >= d)
        def _(d=d):
            copies[d - 1].wait_recv()
            out[2] = (
                tails[d, pl.ds(0, lines), :]
                + jnp.max(tails[d, pl.ds(lines, 8), :], axis=0, keepdims=True) * out[2]
            )

    @pl.when(me < count - 1)
    def _():
        to_right.wait_send()

    @pl.when(me > 0)
    def _():
        to_left.wait_send()

    for d in range(1, count):

        @pl.when(me + d < count)
        def _(d=d):
            copies[d - 1].wait_send()


def loads(coefz):
    width = coefz.shape[1]
    row = lax.broadcasted_iota(jnp.int32, (2 * width, width), 0)
    twice = 2 * lax.broadcasted_iota(jnp.int32, (2 * width, width), 1)
    a, b, half_even, half_odd, a_before, b_before = [coefz[k : k + 1, :] for k in range(6)]
    zero = jnp.zeros((2 * width, width), jnp.float32)
    detail = jnp.where(row == twice, -a, zero)
    detail = jnp.where(row == twice + 1, 1.0, detail)
    detail = jnp.where(row == twice + 2, -b, detail)
    earlier = jnp.where(row == twice - 2, -a_before, zero)
    earlier = jnp.where(row == twice - 1, 1.0, earlier)
    earlier = jnp.where(row == twice, -b_before, earlier)
    return detail, half_even * detail + half_odd * earlier, row == twice


def first_kernel(
    nodes, planes, coefs, factor, gain, coefz, factor_z, gain_z, detail, coarse, payload,
    weights, *, count,
):
    me = lax.axis_index("gx")
    half = detail.shape[0]
    total = count * half

    def coef(row, k):
        return coefs[row * total + me * half + k]

    width = factor_z.shape[0]

    @pl.when(pl.program_id(0) == 0)
    def _():
        load = loads(coefz)[1]
        tail = lax.dot_general(
            factor_z[pl.ds(width - 8, 8), :], load, (((1,), (1,)), ((), ())), precision=HIGHEST
        )
        lane = lax.broadcasted_iota(jnp.int32, (1, 2 * width), 1)
        a_last = coefz[0:1, width - 1 : width]
        weights[...] = jnp.zeros_like(weights)
        weights[0:1, :] = jnp.where(lane == 0, 1.0, 0.0)
        weights[1:2, :] = jnp.where(
            lane == 2 * width - 2, -a_last, jnp.where(lane == 2 * width - 1, 1.0, 0.0)
        )
        weights[2:3, :] = tail[7:8, :]

    for i in range(nodes.shape[1] // 8):
        rows = pl.ds(i * 8, 8)
        even = [nodes[2 * k, rows, :] for k in range(half)]
        before = planes[0, rows, :] - coef(5, 0) * even[0]
        load = []
        for k in range(half):
            after = even[k + 1] if k + 1 < half else planes[1, rows, :]
            value = nodes[2 * k + 1, rows, :] - coef(0, k) * even[k] - coef(1, k) * after
            detail[k, rows, :] = value
            load.append(coef(2, k) * value + coef(3, k) * before)
            before = value
        for k in range(half):
            value = nodes[2 * k, rows, :] + gain[k] * planes[2, rows, :]
            for j in range(half):
                value = value + factor[k, j] * load[j]
            coarse[k, rows, :] = value

    lines = coarse[...].reshape(half * coarse.shape[1], coarse.shape[2])
    sent = lax.dot_general(
        weights[...], lines, (((1,), (1,)), ((), ())), precision=HIGHEST
    )
    kind = lax.broadcasted_iota(jnp.int32, sent.shape, 0)
    end_gain = gain_z[0:1, width - 1 : width]
    end_first = factor_z[width - 1 : width, 0:1] * coefz[3:4, 0:1]
    end_last = -(
        factor_z[width - 1 : width, width - 1 : width]
        * coefz[2:3, width - 1 : width]
        * coefz[1:2, width - 1 : width]
    )
    sent = jnp.where(kind == 3, end_gain, sent)
    sent = jnp.where(kind == 4, end_first, sent)
    sent = jnp.where(kind == 5, end_last, sent)
    payload[0] = sent


def third_kernel(
    placed, coarse, gathered, coefz, factor_z, gain_z, detail, outgoing, matrix, update, tiles,
    *, count, chunks,
):
    me = lax.axis_index("gz")
    step = pl.program_id(0)
    width = factor_z.shape[0]

    @pl.when(step == 0)
    def _():
        outgoing[...] = jnp.zeros_like(outgoing)
        detail_of, load_of, is_even = loads(coefz)
        solved = lax.dot_general(
            load_of, factor_z[...], (((1,), (1,)), ((), ())), precision=HIGHEST
        )
        matrix[:, 0:width] = jnp.where(is_even, 1.0, 0.0) + solved
        matrix[:, width:] = detail_of
        turned = factor_z[...].T
        b_last = coefz[1:2, width - 1 : width]
        lane = lax.broadcasted_iota(jnp.int32, (1, width), 1)
        update[...] = jnp.zeros_like(update)
        update[0:1, 0:width] = -turned[width - 1 : width, :] * (
            coefz[2:3, width - 1 : width] * b_last
        )
        update[0:1, width:] = jnp.where(lane == width - 1, -b_last, 0.0)
        update[1:2, 0:width] = turned[0:1, :] * coefz[3:4, 0:1]
        update[2:3, 0:width] = gain_z[...]

    def heard(p, row):
        return gathered[p, 0, row : row + 1, :]

    empty = jnp.zeros_like(heard(0, 0))
    right, left, carry = empty, empty, empty
    for p in range(count):
        right = jnp.where(me + 1 == p, heard(p, 0), right)
        left = jnp.where(me - 1 == p, heard(p, 1), left)
        if p < count - 1:
            tail = heard(p, 2) + heard(p, 5) * heard(p + 1, 0) + heard(p, 3) * carry
            if p > 0:
                tail = tail + heard(p, 4) * heard(p - 1, 1)
            carry = jnp.where(p < me, tail, carry)
    kind = lax.broadcasted_iota(jnp.int32, (8, empty.shape[1]), 0)
    edges = jnp.where(kind == 0, right, jnp.where(kind == 1, left, jnp.where(kind == 2, carry, 0.0)))

    rows = coarse.shape[0] * coarse.shape[1]
    lines = coarse[...].reshape(rows, coarse.shape[2])
    result = jnp.dot(lines, matrix[...], precision=HIGHEST) + lax.dot_general(
        edges, update[...], (((0,), (0,)), ((), ())), precision=HIGHEST
    )
    upper = result[:, :width].reshape(rows // 8, 8, width)
    lower = result[:, width:].reshape(rows // 8, 8, width)
    detail[...] = result[:, width:].reshape(detail.shape)
    top = lax.broadcasted_iota(jnp.int32, upper.shape, 1) < LINES
    tiles[0] = jnp.where(top, upper, pltpu.roll(lower, LINES, 1))
    tiles[1] = jnp.where(top, pltpu.roll(upper, LINES, 1), lower)
    eights = coarse.shape[1] // 8

    def scatter(x, carry):
        for j in range(eights):
            for half in range(2):
                block = x * (2 * eights * chunks) + step * (2 * eights) + 2 * j + half
                outgoing[placed[block]] = tiles[half, x * eights + j]
        return carry

    lax.fori_loop(0, coarse.shape[0], scatter, 0)


def deliver_kernel(n_gy, n_gz, outgoing, received, send_sem, recv_sem, own_sem):
    gy, gz = lax.axis_index("gy"), lax.axis_index("gz")
    me = gy * n_gz + gz
    shifts = [
        (dy, dz) for dy in range(n_gy) for dz in range(n_gz) if dy + dz > 0
    ]
    shifts.sort(key=lambda shift: -min(shift[0], n_gy - shift[0]))
    barrier = pltpu.get_barrier_semaphore()
    targets = []
    for dy, dz in shifts:
        there = (lax.rem(gy + dy, n_gy), lax.rem(gz + dz, n_gz))
        targets.append(there)
        pl.semaphore_signal(
            barrier, inc=1, device_id={"gy": there[0], "gz": there[1]}, device_id_type=MESH
        )
    own = pltpu.make_async_copy(outgoing.at[me], received.at[me], own_sem)
    own.start()
    pl.semaphore_wait(barrier, len(shifts))
    copies = []
    for k, there in enumerate(targets):
        copy = pltpu.make_async_remote_copy(
            src_ref=outgoing.at[there[0] * n_gz + there[1]],
            dst_ref=received.at[me],
            send_sem=send_sem.at[k],
            recv_sem=recv_sem.at[k],
            device_id={"gy": there[0], "gz": there[1]},
            device_id_type=MESH,
        )
        copy.start()
        copies.append(copy)
    own.wait()
    for copy in copies:
        copy.wait()


def spread_kernel(sent, outgoing, received, lists, send_sem, recv_sem, own_sem):
    gy, gz = lax.axis_index("gy"), lax.axis_index("gz")
    half, place = gy // 2, lax.rem(gy, 2)
    me = gy * 2 + gz
    capacity = received.shape[1]

    def at(step):
        h, y, z = step
        there_half = 1 - half if h else half
        there_place = 1 - place if y else place
        return there_half * 2 + there_place, 1 - gz if z else gz

    steps = [(h, y, z) for h in (0, 1) for y in (0, 1) for z in (0, 1) if h + y + z]
    barrier = pltpu.get_barrier_semaphore()
    for step in steps:
        there = at(step)
        pl.semaphore_signal(
            barrier, inc=1, device_id={"gy": there[0], "gz": there[1]}, device_id_type=MESH
        )
    own = pltpu.make_async_copy(
        outgoing.at[pl.ds(me * capacity, capacity)], received.at[me], own_sem
    )
    own.start()
    pl.semaphore_wait(barrier, len(steps))

    def copy(k, step, source, target):
        there = at(step)
        return pltpu.make_async_remote_copy(
            src_ref=source, dst_ref=target, send_sem=send_sem.at[k], recv_sem=recv_sem.at[k],
            device_id={"gy": there[0], "gz": there[1]}, device_id_type=MESH,
        )

    def direct(step):
        there = at(step)
        count = capacity // 2 if step[0] else capacity
        return copy(
            steps.index(step), step,
            outgoing.at[pl.ds((there[0] * 2 + there[1]) * capacity, count)],
            received.at[me, pl.ds(0, count)],
        )

    mine, beside = place * 2 + gz, (1 - place) * 2 + gz
    rows = pl.ds(0, sent)
    tail = pl.ds(received.shape[0] * capacity, sent)
    across = copy(7, (1, 0, 0), outgoing.at[tail], lists.at[mine, rows])
    along = copy(8, (0, 1, 0), lists.at[mine, rows], lists.at[mine, rows])
    to_core = copy(9, (0, 0, 1), lists.at[mine, rows], lists.at[mine, rows])
    to_core_too = copy(10, (0, 0, 1), lists.at[beside, rows], lists.at[beside, rows])
    early = [direct((0, 1, 0)), direct((0, 0, 1))]
    late = [direct(step) for step in ((1, 0, 0), (1, 0, 1), (1, 1, 0), (1, 1, 1), (0, 1, 1))]
    across.start()
    for one in early:
        one.start()
    across.wait_recv()
    along.start()
    to_core.start()
    for one in late:
        one.start()
    along.wait_recv()
    to_core_too.start()
    own.wait()
    across.wait_send()
    along.wait_send()
    for one in early + late + [to_core, to_core_too]:
        one.wait()


def gather_kernel(counts, place, base, lists, received):
    step = pl.program_id(0)
    capacity = base.shape[1]
    direct = capacity // 2
    me = place[1]
    half = me // 4
    sender = place[0] * 8 + lax.rem(step + 4 * (1 - half), 8)
    received[...] = base[...]

    @pl.when(step < 4)
    def _():
        start = jnp.int32(0)
        for k in range(4):
            more = jnp.maximum(counts[sender * 8 + half * 4 + k] - direct, 0)
            start = start + jnp.where(half * 4 + k < me, more, 0)
        count = jnp.maximum(counts[sender * 8 + me] - direct, 0)
        tiles = lists[0, pl.ds(start, direct)]
        slot = lax.broadcasted_iota(jnp.int32, tiles.shape, 0)
        received[0, pl.ds(direct, direct)] = jnp.where(slot < count, tiles, 0.0)


def spread(outgoing, group, room, counts, levels, needed):
    capacity = (outgoing.shape[0] - room) // group
    tile = outgoing.shape[1:]

    def branch(number, sent):
        def run(outgoing):
            return pl.pallas_call(
                functools.partial(spread_kernel, sent),
                out_shape=[
                    jax.ShapeDtypeStruct((group, capacity) + tile, jnp.float32),
                    jax.ShapeDtypeStruct((group // 2, room) + tile, jnp.float32),
                ],
                in_specs=[pl.BlockSpec(memory_space=pl.ANY)],
                out_specs=[pl.BlockSpec(memory_space=pl.ANY)] * 2,
                scratch_shapes=[
                    pltpu.SemaphoreType.DMA((11,)),
                    pltpu.SemaphoreType.DMA((11,)),
                    pltpu.SemaphoreType.DMA,
                ],
                compiler_params=pltpu.CompilerParams(
                    collective_id=2 + number, has_side_effects=True
                ),
                name="spread",
            )(outgoing)

        return run

    branches = [branch(k, sent) for k, sent in enumerate(levels + (room,))]
    level = sum((needed > sent).astype(jnp.int32) for sent in levels)
    base, lists = lax.switch(level, branches, outgoing)
    place = jnp.stack(
        [lax.axis_index("gx"), lax.axis_index("gy") * 2 + lax.axis_index("gz")]
    ).astype(jnp.int32)
    rows, width = tile

    def sender(i, counts, place):
        return lax.rem(i + 4 * (1 - place[1] // 4), 8), 0, 0, 0

    return pl.pallas_call(
        gather_kernel,
        grid_spec=pltpu.PrefetchScalarGridSpec(
            num_scalar_prefetch=2,
            grid=(group,),
            in_specs=[
                pl.BlockSpec((1, capacity, rows, width), sender),
                pl.BlockSpec(
                    (1, room, rows, width), lambda i, counts, place: (jnp.minimum(i, 3), 0, 0, 0)
                ),
            ],
            out_specs=pl.BlockSpec((1, capacity, rows, width), sender),
        ),
        out_shape=jax.ShapeDtypeStruct(base.shape, jnp.float32),
        compiler_params=pltpu.CompilerParams(
            dimension_semantics=("arbitrary",), vmem_limit_bytes=LIMIT
        ),
        name="gather",
    )(counts, place, base, lists)


def local(sizes, nodes, spacing_x, spacing_z, factor_x, gain_x, factor_z, gain_z, receivers):
    n_gx, n_gy, n_gz = sizes
    length, lines, depth = nodes.shape
    half, width = length // 2, depth // 2
    coefs = coefficients(spacing_x).reshape(-1)
    coefz = lax.dynamic_slice_in_dim(
        coefficients(spacing_z), lax.axis_index("gz") * width, width, axis=1
    )
    gain_row = gain_z.reshape(1, width)
    vmem = pl.BlockSpec(memory_space=pltpu.VMEM)
    smem = pl.BlockSpec(memory_space=pltpu.SMEM)
    hbm = pl.BlockSpec(memory_space=pl.ANY)

    def exchange(nodes, coefs, factor, gain, out, left, right, send, tails, s_sem, r_sem):
        exchange_first(
            n_gx, nodes, coefs, factor, gain, out, left, right, send, tails, (s_sem, r_sem)
        )

    planes = pl.pallas_call(
        exchange,
        out_shape=jax.ShapeDtypeStruct((3, lines, depth), jnp.float32),
        in_specs=[vmem, smem, smem, smem],
        out_specs=vmem,
        scratch_shapes=[
            pltpu.VMEM((lines, depth), jnp.float32),
            pltpu.VMEM((lines, depth), jnp.float32),
            pltpu.VMEM((2, lines + 8, depth), jnp.float32),
            pltpu.VMEM((n_gx, lines + 8, depth), jnp.float32),
            pltpu.SemaphoreType.DMA((n_gx + 1,)),
            pltpu.SemaphoreType.DMA((n_gx + 1,)),
        ],
        compiler_params=pltpu.CompilerParams(
            collective_id=0, has_side_effects=True, vmem_limit_bytes=LIMIT
        ),
        name="exchange_first",
    )(nodes, coefs, factor_x, gain_x)

    chunks = 4
    rows = lines // chunks
    params = pltpu.CompilerParams(
        dimension_semantics=("arbitrary",), vmem_limit_bytes=LIMIT
    )
    detail_x, coarse_x, payload = pl.pallas_call(
        functools.partial(first_kernel, count=n_gx),
        grid=(chunks,),
        in_specs=[
            pl.BlockSpec((length, rows, depth), lambda i: (0, i, 0)),
            pl.BlockSpec((3, rows, depth), lambda i: (0, i, 0)),
            smem, smem, smem,
            pl.BlockSpec((8, width), lambda i: (0, 0)),
            pl.BlockSpec((width, width), lambda i: (0, 0)),
            pl.BlockSpec((1, width), lambda i: (0, 0)),
        ],
        out_specs=[
            pl.BlockSpec((half, rows, depth), lambda i: (0, i, 0)),
            pl.BlockSpec((half, rows, depth), lambda i: (0, i, 0)),
            pl.BlockSpec((1, 8, half * rows), lambda i: (i, 0, 0)),
        ],
        out_shape=[
            jax.ShapeDtypeStruct((half, lines, depth), jnp.float32),
            jax.ShapeDtypeStruct((half, lines, depth), jnp.float32),
            jax.ShapeDtypeStruct((chunks, 8, half * rows), jnp.float32),
        ],
        scratch_shapes=[pltpu.VMEM((8, depth), jnp.float32)],
        compiler_params=params,
        name="pass_first",
    )(nodes, planes, coefs, factor_x, gain_x, coefz, factor_z, gain_row)

    gathered = lax.all_gather(payload, "gz")

    blocks = half * lines // LINES
    group = n_gy * n_gz
    capacity = max(2, blocks // group * 2)
    targets = receivers[:, 0]
    positions = jnp.arange(blocks, dtype=jnp.int32)
    earlier = (targets[None, :] == targets[:, None]) & (positions[None, :] < positions[:, None])
    slots = jnp.sum(earlier.astype(jnp.int32), axis=1)
    placed = targets * capacity + slots
    listed = n_gy == 4 and n_gz == 2
    room = 0
    if listed:
        direct = capacity // 2
        room = group // 2 * (capacity - direct)
        there = 1 - lax.axis_index("gy") // 2
        members = jnp.arange(group, dtype=jnp.int32)
        tally = jnp.sum((targets[:, None] == members[None, :]).astype(jnp.int32), axis=0)
        more = jnp.where(members // 4 == there, jnp.maximum(tally - direct, 0), 0)
        before = jnp.sum(jnp.where(members[None, :] < targets[:, None], more[None, :], 0), axis=1)
        placed = jnp.where(
            (targets // 4 == there) & (slots >= direct),
            group * capacity + before + slots - direct,
            placed,
        )
        tallies = lax.all_gather(tally, ("gx", "gy", "gz"))
        senders = jnp.arange(tallies.shape[0], dtype=jnp.int32) % group
        crossing = senders[:, None] // 4 != members[None, :] // 4
        needed = jnp.max(
            jnp.sum(jnp.where(crossing, jnp.maximum(tallies - direct, 0), 0), axis=1)
        )

    held = group * capacity + room
    detail_z, outgoing = pl.pallas_call(
        functools.partial(third_kernel, count=n_gz, chunks=chunks),
        grid=(chunks,),
        in_specs=[
            smem,
            pl.BlockSpec((half, rows, depth), lambda i: (0, i, 0)),
            pl.BlockSpec((n_gz, 1, 8, half * rows), lambda i: (0, i, 0, 0)),
            pl.BlockSpec((8, width), lambda i: (0, 0)),
            pl.BlockSpec((width, width), lambda i: (0, 0)),
            pl.BlockSpec((1, width), lambda i: (0, 0)),
        ],
        out_specs=[
            pl.BlockSpec((half, rows, width), lambda i: (0, i, 0)),
            pl.BlockSpec((held, 2 * LINES, width), lambda i: (0, 0, 0)),
        ],
        out_shape=[
            jax.ShapeDtypeStruct((half, lines, width), jnp.float32),
            jax.ShapeDtypeStruct((held, 2 * LINES, width), jnp.float32),
        ],
        scratch_shapes=[
            pltpu.VMEM((depth, depth), jnp.float32),
            pltpu.VMEM((8, depth), jnp.float32),
            pltpu.VMEM((2, half * rows // 8, 8, width), jnp.float32),
        ],
        compiler_params=params,
        name="pass_third",
    )(placed, coarse_x, gathered, coefz, factor_z, gain_row)

    if listed:
        levels = (room * 3 // 8, room // 2, room * 5 // 8)
        received = spread(outgoing, group, room, tallies.reshape(-1), levels, needed)
    else:
        outgoing = outgoing.reshape(group, capacity, 2 * LINES, width)
        received = pl.pallas_call(
            functools.partial(deliver_kernel, n_gy, n_gz),
            out_shape=jax.ShapeDtypeStruct(outgoing.shape, jnp.float32),
            in_specs=[hbm],
            out_specs=hbm,
            scratch_shapes=[
                pltpu.SemaphoreType.DMA((group - 1,)),
                pltpu.SemaphoreType.DMA((group - 1,)),
                pltpu.SemaphoreType.DMA,
            ],
            compiler_params=pltpu.CompilerParams(collective_id=1, has_side_effects=True),
            name="deliver",
        )(outgoing)
    return (
        detail_x,
        detail_z,
        received.reshape(1, group, capacity, 2, LINES, width),
    )


def solution(mesh):
    sizes = tuple(mesh.shape[axis] for axis in ("gx", "gy", "gz"))
    return jax.shard_map(
        functools.partial(local, sizes),
        mesh=mesh,
        in_specs=(
            P("gx", "gy", "gz"),
            P(),
            P(),
            P("gx", None),
            P("gx"),
            P("gz", None),
            P("gz"),
            P(("gx", "gy", "gz"), None),
        ),
        out_specs=(
            P("gx", "gy", "gz"),
            P("gx", "gy", "gz"),
            P(("gx", "gy", "gz"), None, None, None, None, None),
        ),
        check_vma=False,
    )
```

```python
import functools

import jax
import jax.numpy as jnp
from jax import lax
from jax.experimental import pallas as pl
from jax.experimental.pallas import tpu as pltpu
from jax.sharding import PartitionSpec as P

LINES = 4
MESH = pl.DeviceIdType.MESH
HIGHEST = lax.Precision.HIGHEST
LIMIT = 56 * 1024 * 1024


def coefficients(spacing):
    even, odd = spacing[0::2], spacing[1::2]
    total = even + odd
    a, b = odd / total, even / total

    def before(row):
        return jnp.concatenate([jnp.zeros_like(row[:1]), row[:-1]])

    zero = jnp.zeros_like(a)
    return jnp.stack(
        [a, b, 0.5 * even, before(0.5 * odd), before(a), before(b), zero, zero]
    )


class Table:
    def __init__(self, scalars, start, side):
        self.scalars, self.start, self.side = scalars, start, side

    def __getitem__(self, place):
        return self.scalars[self.start + place[0] * self.side + place[1]]


def exchange_first(
    count, over, scalars, hbm_nodes, out, most, nodes, left, right, send, tails, needs, wants,
    send_sem, recv_sem, need_send, need_recv, want_send, want_recv, load_sem,
):
    me, row = lax.axis_index("gx"), lax.axis_index("gy")
    load = pltpu.make_async_copy(hbm_nodes, nodes, load_sem)
    load.start()
    half = nodes.shape[0] // 2
    lines = nodes.shape[1]
    total = count * half
    barrier = pltpu.get_barrier_semaphore()
    for d in range(1, count):
        pl.semaphore_signal(
            barrier, inc=1, device_id={"gx": lax.rem(me + d, count)}, device_id_type=MESH
        )
    for d in range(1, over):
        pl.semaphore_signal(
            barrier, inc=1, device_id={"gy": lax.rem(row + d, over)}, device_id_type=MESH
        )

    def coef(kind, k):
        return scalars[kind * total + me * half + k]

    factor = Table(scalars, 8 * total, half)
    gain_last = scalars[8 * total + half * half + half - 1]
    needs[0] = jnp.full(needs.shape[1:], scalars[8 * total + half * half + half], jnp.float32)
    load.wait()

    last = half - 1
    send[1, pl.ds(0, lines), :] = nodes[2 * last + 1] - coef(0, last) * nodes[2 * last]
    pl.semaphore_wait(barrier, count + over - 2)

    to_right = pltpu.make_async_remote_copy(
        src_ref=send.at[1, pl.ds(0, lines)], dst_ref=left, send_sem=send_sem.at[0], recv_sem=recv_sem.at[0],
        device_id={"gx": lax.rem(me + 1, count)}, device_id_type=MESH,
    )
    to_left = pltpu.make_async_remote_copy(
        src_ref=nodes.at[0], dst_ref=right, send_sem=send_sem.at[1], recv_sem=recv_sem.at[1],
        device_id={"gx": lax.rem(me + count - 1, count)}, device_id_type=MESH,
    )

    @pl.when(me < count - 1)
    def _():
        to_right.start()

    @pl.when(me > 0)
    def _():
        to_left.start()

    small = []
    for d in range(1, count):
        small.append(
            pltpu.make_async_remote_copy(
                src_ref=needs.at[0], dst_ref=needs.at[d],
                send_sem=need_send.at[d], recv_sem=need_recv.at[d],
                device_id={"gx": lax.rem(me + d, count)}, device_id_type=MESH,
            )
        )
        small[-1].start()

    weights = []
    for k in range(half):
        weight = factor[last, k] * coef(2, k)
        if k < last:
            weight = weight + factor[last, k + 1] * coef(3, k + 1)
        weights.append(weight)
    edge = factor[last, 0] * coef(3, 0)

    def chunk(i, carry):
        rows = pl.ds(pl.multiple_of(i * 8, 8), 8)
        even = nodes[0, rows, :]
        value = (-edge * coef(5, 0)) * even
        for k in range(half):
            detail = nodes[2 * k + 1, rows, :] - coef(0, k) * even
            if k < last:
                even = nodes[2 * k + 2, rows, :]
                detail = detail - coef(1, k) * even
            value = value + weights[k] * detail
        send[0, rows, :] = value
        return carry

    lax.fori_loop(0, lines // 8, chunk, 0)
    for one in small:
        one.wait_recv()
    wants[0] = jnp.max(needs[...], axis=0)
    for d in range(1, over):
        small.append(
            pltpu.make_async_remote_copy(
                src_ref=wants.at[0], dst_ref=wants.at[d],
                send_sem=want_send.at[d], recv_sem=want_recv.at[d],
                device_id={"gy": lax.rem(row + d, over)}, device_id_type=MESH,
            )
        )
        small[-1].start()

    @pl.when(me == 0)
    def _():
        left[...] = jnp.zeros_like(left)

    @pl.when(me == count - 1)
    def _():
        right[...] = jnp.zeros_like(right)

    @pl.when(me > 0)
    def _():
        to_right.wait_recv()

    @pl.when(me < count - 1)
    def _():
        to_left.wait_recv()

    end = -(factor[last, last] * coef(2, last)) * coef(1, last)
    own = send.at[0]
    own[pl.ds(0, lines), :] = own[pl.ds(0, lines), :] + edge * left[...] + end * right[...]
    own[pl.ds(lines, 8), :] = jnp.full((8, own.shape[1]), gain_last, jnp.float32)

    copies = []
    for d in range(1, count):
        copies.append(
            pltpu.make_async_remote_copy(
                src_ref=tails.at[0], dst_ref=tails.at[d],
                send_sem=send_sem.at[1 + d], recv_sem=recv_sem.at[1 + d],
                device_id={"gx": lax.rem(me + d, count)}, device_id_type=MESH,
            )
        )
    tails[0] = own[...]
    for d in range(1, count):

        @pl.when(me + d < count)
        def _(d=d):
            copies[d - 1].start()

    out[0] = left[...]
    out[1] = right[...]
    out[2] = jnp.zeros_like(left)
    for d in range(count - 1, 0, -1):

        @pl.when(me >= d)
        def _(d=d):
            copies[d - 1].wait_recv()
            out[2] = (
                tails[d, pl.ds(0, lines), :]
                + jnp.max(tails[d, pl.ds(lines, 8), :], axis=0, keepdims=True) * out[2]
            )

    for one in small[count - 1 :]:
        one.wait_recv()
    most[...] = jnp.max(wants[...], axis=0)
    for one in small:
        one.wait_send()

    @pl.when(me < count - 1)
    def _():
        to_right.wait_send()

    @pl.when(me > 0)
    def _():
        to_left.wait_send()

    for d in range(1, count):

        @pl.when(me + d < count)
        def _(d=d):
            copies[d - 1].wait_send()


def loads(coefz):
    width = coefz.shape[1]
    row = lax.broadcasted_iota(jnp.int32, (2 * width, width), 0)
    twice = 2 * lax.broadcasted_iota(jnp.int32, (2 * width, width), 1)
    a, b, half_even, half_odd, a_before, b_before = [coefz[k : k + 1, :] for k in range(6)]
    zero = jnp.zeros((2 * width, width), jnp.float32)
    detail = jnp.where(row == twice, -a, zero)
    detail = jnp.where(row == twice + 1, 1.0, detail)
    detail = jnp.where(row == twice + 2, -b, detail)
    earlier = jnp.where(row == twice - 2, -a_before, zero)
    earlier = jnp.where(row == twice - 1, 1.0, earlier)
    earlier = jnp.where(row == twice, -b_before, earlier)
    return detail, half_even * detail + half_odd * earlier, row == twice


def first_kernel(
    nodes, planes, most, scalars, coefz, factor_z, gain_z, detail, coarse, payload, weights,
    *, count,
):
    me = lax.axis_index("gx")
    half = detail.shape[0]
    total = count * half
    factor = Table(scalars, 8 * total, half)

    def coef(row, k):
        return scalars[row * total + me * half + k]

    width = factor_z.shape[0]

    @pl.when(pl.program_id(0) == 0)
    def _():
        load = loads(coefz)[1]
        tail = lax.dot_general(
            factor_z[pl.ds(width - 8, 8), :], load, (((1,), (1,)), ((), ())), precision=HIGHEST
        )
        lane = lax.broadcasted_iota(jnp.int32, (1, 2 * width), 1)
        a_last = coefz[0:1, width - 1 : width]
        weights[...] = jnp.zeros_like(weights)
        weights[0:1, :] = jnp.where(lane == 0, 1.0, 0.0)
        weights[1:2, :] = jnp.where(
            lane == 2 * width - 2, -a_last, jnp.where(lane == 2 * width - 1, 1.0, 0.0)
        )
        weights[2:3, :] = tail[7:8, :]

    for i in range(nodes.shape[1] // 8):
        rows = pl.ds(i * 8, 8)
        even = [nodes[2 * k, rows, :] for k in range(half)]
        before = planes[0, rows, :] - coef(5, 0) * even[0]
        load = []
        for k in range(half):
            after = even[k + 1] if k + 1 < half else planes[1, rows, :]
            value = nodes[2 * k + 1, rows, :] - coef(0, k) * even[k] - coef(1, k) * after
            detail[k, rows, :] = value
            load.append(coef(2, k) * value + coef(3, k) * before)
            before = value
        for k in range(half):
            value = nodes[2 * k, rows, :] + scalars[8 * total + half * half + k] * planes[2, rows, :]
            for j in range(half):
                value = value + factor[k, j] * load[j]
            coarse[k, rows, :] = value

    lines = coarse[...].reshape(half * coarse.shape[1], coarse.shape[2])
    sent = lax.dot_general(
        weights[...], lines, (((1,), (1,)), ((), ())), precision=HIGHEST
    )
    kind = lax.broadcasted_iota(jnp.int32, sent.shape, 0)
    end_gain = gain_z[0:1, width - 1 : width]
    end_first = factor_z[width - 1 : width, 0:1] * coefz[3:4, 0:1]
    end_last = -(
        factor_z[width - 1 : width, width - 1 : width]
        * coefz[2:3, width - 1 : width]
        * coefz[1:2, width - 1 : width]
    )
    sent = jnp.where(kind == 3, end_gain, sent)
    sent = jnp.where(kind == 4, end_first, sent)
    sent = jnp.where(kind == 5, end_last, sent)
    sent = jnp.where(kind == 6, most[0:1, 0:1], sent)
    payload[0] = sent


def third_kernel(
    placed, coarse, gathered, coefz, factor_z, gain_z, header, detail, outgoing, level, matrix,
    update, tiles, *, count, chunks, levels, head,
):
    me = lax.axis_index("gz")
    step = pl.program_id(0)
    width = factor_z.shape[0]

    @pl.when(step == 0)
    def _():
        outgoing[...] = jnp.zeros_like(outgoing)
        outgoing[head] = header[...]
        need = jnp.max(gathered[:, 0, 6:7, :])
        level[0] = sum((need > sent).astype(jnp.int32) for sent in levels)
        detail_of, load_of, is_even = loads(coefz)
        solved = lax.dot_general(
            load_of, factor_z[...], (((1,), (1,)), ((), ())), precision=HIGHEST
        )
        matrix[:, 0:width] = jnp.where(is_even, 1.0, 0.0) + solved
        matrix[:, width:] = detail_of
        turned = factor_z[...].T
        b_last = coefz[1:2, width - 1 : width]
        lane = lax.broadcasted_iota(jnp.int32, (1, width), 1)
        update[...] = jnp.zeros_like(update)
        update[0:1, 0:width] = -turned[width - 1 : width, :] * (
            coefz[2:3, width - 1 : width] * b_last
        )
        update[0:1, width:] = jnp.where(lane == width - 1, -b_last, 0.0)
        update[1:2, 0:width] = turned[0:1, :] * coefz[3:4, 0:1]
        update[2:3, 0:width] = gain_z[...]

    def heard(p, row):
        return gathered[p, 0, row : row + 1, :]

    empty = jnp.zeros_like(heard(0, 0))
    right, left, carry = empty, empty, empty
    for p in range(count):
        right = jnp.where(me + 1 == p, heard(p, 0), right)
        left = jnp.where(me - 1 == p, heard(p, 1), left)
        if p < count - 1:
            tail = heard(p, 2) + heard(p, 5) * heard(p + 1, 0) + heard(p, 3) * carry
            if p > 0:
                tail = tail + heard(p, 4) * heard(p - 1, 1)
            carry = jnp.where(p < me, tail, carry)
    kind = lax.broadcasted_iota(jnp.int32, (8, empty.shape[1]), 0)
    edges = jnp.where(kind == 0, right, jnp.where(kind == 1, left, jnp.where(kind == 2, carry, 0.0)))

    rows = coarse.shape[0] * coarse.shape[1]
    lines = coarse[...].reshape(rows, coarse.shape[2])
    result = jnp.dot(lines, matrix[...], precision=HIGHEST) + lax.dot_general(
        edges, update[...], (((0,), (0,)), ((), ())), precision=HIGHEST
    )
    upper = result[:, :width].reshape(rows // 8, 8, width)
    lower = result[:, width:].reshape(rows // 8, 8, width)
    detail[...] = result[:, width:].reshape(detail.shape)
    top = lax.broadcasted_iota(jnp.int32, upper.shape, 1) < LINES
    tiles[0] = jnp.where(top, upper, pltpu.roll(lower, LINES, 1))
    tiles[1] = jnp.where(top, pltpu.roll(upper, LINES, 1), lower)
    eights = coarse.shape[1] // 8

    def scatter(x, carry):
        for j in range(eights):
            for half in range(2):
                block = x * (2 * eights * chunks) + step * (2 * eights) + 2 * j + half
                outgoing[placed[block]] = tiles[half, x * eights + j]
        return carry

    lax.fori_loop(0, coarse.shape[0], scatter, 0)


def deliver_kernel(n_gy, n_gz, outgoing, received, send_sem, recv_sem, own_sem):
    gy, gz = lax.axis_index("gy"), lax.axis_index("gz")
    me = gy * n_gz + gz
    shifts = [
        (dy, dz) for dy in range(n_gy) for dz in range(n_gz) if dy + dz > 0
    ]
    shifts.sort(key=lambda shift: -min(shift[0], n_gy - shift[0]))
    barrier = pltpu.get_barrier_semaphore()
    targets = []
    for dy, dz in shifts:
        there = (lax.rem(gy + dy, n_gy), lax.rem(gz + dz, n_gz))
        targets.append(there)
        pl.semaphore_signal(
            barrier, inc=1, device_id={"gy": there[0], "gz": there[1]}, device_id_type=MESH
        )
    own = pltpu.make_async_copy(outgoing.at[me], received.at[me], own_sem)
    own.start()
    pl.semaphore_wait(barrier, len(shifts))
    copies = []
    for k, there in enumerate(targets):
        copy = pltpu.make_async_remote_copy(
            src_ref=outgoing.at[there[0] * n_gz + there[1]],
            dst_ref=received.at[me],
            send_sem=send_sem.at[k],
            recv_sem=recv_sem.at[k],
            device_id={"gy": there[0], "gz": there[1]},
            device_id_type=MESH,
        )
        copy.start()
        copies.append(copy)
    own.wait()
    for copy in copies:
        copy.wait()


def spread_kernel(sent, outgoing, received, lists, send_sem, recv_sem, own_sem):
    gy, gz = lax.axis_index("gy"), lax.axis_index("gz")
    half, place = gy // 2, lax.rem(gy, 2)
    me = gy * 2 + gz
    capacity = received.shape[1]

    def at(step):
        h, y, z = step
        there_half = 1 - half if h else half
        there_place = 1 - place if y else place
        return there_half * 2 + there_place, 1 - gz if z else gz

    steps = [(h, y, z) for h in (0, 1) for y in (0, 1) for z in (0, 1) if h + y + z]
    barrier = pltpu.get_barrier_semaphore()
    for step in steps:
        there = at(step)
        pl.semaphore_signal(
            barrier, inc=1, device_id={"gy": there[0], "gz": there[1]}, device_id_type=MESH
        )
    own = pltpu.make_async_copy(
        outgoing.at[pl.ds(me * capacity, capacity)], received.at[me], own_sem
    )
    own.start()
    pl.semaphore_wait(barrier, len(steps))

    def copy(k, step, source, target):
        there = at(step)
        return pltpu.make_async_remote_copy(
            src_ref=source, dst_ref=target, send_sem=send_sem.at[k], recv_sem=recv_sem.at[k],
            device_id={"gy": there[0], "gz": there[1]}, device_id_type=MESH,
        )

    def direct(step):
        there = at(step)
        count = capacity // 2 if step[0] else capacity
        return copy(
            steps.index(step), step,
            outgoing.at[pl.ds((there[0] * 2 + there[1]) * capacity, count)],
            received.at[me, pl.ds(0, count)],
        )

    mine, beside = place * 2 + gz, (1 - place) * 2 + gz
    rows = pl.ds(0, 1 + sent)
    tail = pl.ds(received.shape[0] * capacity, 1 + sent)
    across = copy(7, (1, 0, 0), outgoing.at[tail], lists.at[mine, rows])
    along = copy(8, (0, 1, 0), lists.at[mine, rows], lists.at[mine, rows])
    to_core = copy(9, (0, 0, 1), lists.at[mine, rows], lists.at[mine, rows])
    to_core_too = copy(10, (0, 0, 1), lists.at[beside, rows], lists.at[beside, rows])
    early = [direct((0, 1, 0)), direct((0, 0, 1))]
    late = [direct(step) for step in ((1, 0, 0), (1, 0, 1), (1, 1, 0), (1, 1, 1), (0, 1, 1))]
    across.start()
    for one in early:
        one.start()
    across.wait_recv()
    along.start()
    to_core.start()
    for one in late:
        one.start()
    along.wait_recv()
    to_core_too.start()
    own.wait()
    across.wait_send()
    along.wait_send()
    for one in early + late + [to_core, to_core_too]:
        one.wait()


def gather_kernel(sent, place, low, high, hbm_lists, received, lists, sems):
    step = pl.program_id(0)
    direct = low.shape[1]
    rows = pl.ds(0, 1 + sent)
    copies = [
        pltpu.make_async_copy(hbm_lists.at[k, rows], lists.at[k, rows], sems.at[k])
        for k in range(4)
    ]

    @pl.when(step == 0)
    def _():
        for one in copies:
            one.start()

    received[0, pl.ds(0, direct)] = low[0]

    @pl.when(step < 4)
    def _():
        received[0, pl.ds(direct, direct)] = high[0]

    me = place[0]
    first = me // 4 * 4
    for k in range(4):

        @pl.when(step == 4 + k)
        def _(k=k):
            copies[k].wait()
            header = lists[k, 0, 0:1, :]
            lane = lax.broadcasted_iota(jnp.int32, header.shape, 1)
            start = jnp.sum(jnp.where((lane >= first) & (lane < me), header, 0.0))
            count = jnp.sum(jnp.where(lane == me, header, 0.0)).astype(jnp.int32)
            tiles = lists[k, pl.ds(1 + start.astype(jnp.int32), direct)]
            slot = lax.broadcasted_iota(jnp.int32, tiles.shape, 0)
            received[0, pl.ds(direct, direct)] = jnp.where(slot < count, tiles, 0.0)


def spread(outgoing, group, room, levels, level):
    capacity = (outgoing.shape[0] - room - 1) // group
    tile = outgoing.shape[1:]
    rows, width = tile
    direct = capacity // 2
    place = (lax.axis_index("gy") * 2 + lax.axis_index("gz")).astype(jnp.int32).reshape(1)

    def sender(i, place):
        return lax.rem(i // 4 * 4 + place[0] // 4 * 4, 8) + lax.rem(i, 4)

    def low_block(i, place):
        return sender(i, place), 0, 0, 0

    def high_block(i, place):
        return sender(jnp.minimum(i, 3), place), 1, 0, 0

    def branch(number, sent):
        def run(outgoing, place):
            base, lists = pl.pallas_call(
                functools.partial(spread_kernel, sent),
                out_shape=[
                    jax.ShapeDtypeStruct((group, capacity) + tile, jnp.float32),
                    jax.ShapeDtypeStruct((group // 2, room + 1) + tile, jnp.float32),
                ],
                in_specs=[pl.BlockSpec(memory_space=pl.ANY)],
                out_specs=[pl.BlockSpec(memory_space=pl.ANY)] * 2,
                scratch_shapes=[
                    pltpu.SemaphoreType.DMA((11,)),
                    pltpu.SemaphoreType.DMA((11,)),
                    pltpu.SemaphoreType.DMA,
                ],
                compiler_params=pltpu.CompilerParams(
                    collective_id=2 + number, has_side_effects=True
                ),
                name="spread",
            )(outgoing)
            return pl.pallas_call(
                functools.partial(gather_kernel, sent),
                grid_spec=pltpu.PrefetchScalarGridSpec(
                    num_scalar_prefetch=1,
                    grid=(group,),
                    in_specs=[
                        pl.BlockSpec((1, direct, rows, width), low_block),
                        pl.BlockSpec((1, direct, rows, width), high_block),
                        pl.BlockSpec(memory_space=pl.ANY),
                    ],
                    out_specs=pl.BlockSpec((1, capacity, rows, width), low_block),
                    scratch_shapes=[
                        pltpu.VMEM((group // 2, room + 1, rows, width), jnp.float32),
                        pltpu.SemaphoreType.DMA((group // 2,)),
                    ],
                ),
                out_shape=jax.ShapeDtypeStruct(base.shape, jnp.float32),
                compiler_params=pltpu.CompilerParams(
                    dimension_semantics=("arbitrary",), vmem_limit_bytes=LIMIT
                ),
                name="gather",
            )(place, base, base, lists)

        return run

    branches = [branch(k, sent) for k, sent in enumerate(levels + (room,))]
    return lax.switch(level, branches, outgoing, place)


def local(sizes, nodes, spacing_x, spacing_z, factor_x, gain_x, factor_z, gain_z, receivers):
    n_gx, n_gy, n_gz = sizes
    length, lines, depth = nodes.shape
    half, width = length // 2, depth // 2
    group = n_gy * n_gz
    blocks = half * lines // LINES
    capacity = max(2, blocks // group * 2)
    listed = n_gy == 4 and n_gz == 2
    direct = capacity // 2
    room = group // 2 * (capacity - direct) if listed else 0
    levels = (room * 3 // 8, room // 2, room * 5 // 8)
    targets = receivers[:, 0]
    positions = jnp.arange(blocks, dtype=jnp.int32)
    earlier = (targets[None, :] == targets[:, None]) & (positions[None, :] < positions[:, None])
    slots = jnp.sum(earlier.astype(jnp.int32), axis=1)
    placed = targets * capacity + slots
    header = jnp.zeros((2 * LINES, width), jnp.float32)
    need = jnp.zeros((1,), jnp.float32)
    if listed:
        there = 1 - lax.axis_index("gy") // 2
        members = jnp.arange(width, dtype=jnp.int32)
        tally = jnp.sum((targets[:, None] == members[None, :]).astype(jnp.int32), axis=0)
        more = jnp.where(members // 4 == there, jnp.maximum(tally - direct, 0), 0)
        before = jnp.sum(jnp.where(members[None, :] < targets[:, None], more[None, :], 0), axis=1)
        placed = jnp.where(
            (targets // 4 == there) & (slots >= direct),
            group * capacity + 1 + before + slots - direct,
            placed,
        )
        header = jnp.broadcast_to(more.astype(jnp.float32)[None, :], header.shape)
        need = jnp.sum(more).astype(jnp.float32).reshape(1)
    scalars = jnp.concatenate(
        [coefficients(spacing_x).reshape(-1), factor_x.reshape(-1), gain_x, need]
    )
    coefz = lax.dynamic_slice_in_dim(
        coefficients(spacing_z), lax.axis_index("gz") * width, width, axis=1
    )
    gain_row = gain_z.reshape(1, width)
    vmem = pl.BlockSpec(memory_space=pltpu.VMEM)
    smem = pl.BlockSpec(memory_space=pltpu.SMEM)
    hbm = pl.BlockSpec(memory_space=pl.ANY)

    planes, most = pl.pallas_call(
        functools.partial(exchange_first, n_gx, n_gy),
        out_shape=[
            jax.ShapeDtypeStruct((3, lines, depth), jnp.float32),
            jax.ShapeDtypeStruct((8, 128), jnp.float32),
        ],
        in_specs=[smem, hbm],
        out_specs=[vmem, vmem],
        scratch_shapes=[
            pltpu.VMEM((length, lines, depth), jnp.float32),
            pltpu.VMEM((lines, depth), jnp.float32),
            pltpu.VMEM((lines, depth), jnp.float32),
            pltpu.VMEM((2, lines + 8, depth), jnp.float32),
            pltpu.VMEM((n_gx, lines + 8, depth), jnp.float32),
            pltpu.VMEM((n_gx, 8, 128), jnp.float32),
            pltpu.VMEM((n_gy, 8, 128), jnp.float32),
            pltpu.SemaphoreType.DMA((n_gx + 1,)),
            pltpu.SemaphoreType.DMA((n_gx + 1,)),
            pltpu.SemaphoreType.DMA((n_gx,)),
            pltpu.SemaphoreType.DMA((n_gx,)),
            pltpu.SemaphoreType.DMA((n_gy,)),
            pltpu.SemaphoreType.DMA((n_gy,)),
            pltpu.SemaphoreType.DMA,
        ],
        compiler_params=pltpu.CompilerParams(
            collective_id=0, has_side_effects=True, vmem_limit_bytes=LIMIT
        ),
        name="exchange_first",
    )(scalars, nodes)

    chunks = 4
    rows = lines // chunks
    params = pltpu.CompilerParams(
        dimension_semantics=("arbitrary",), vmem_limit_bytes=LIMIT
    )
    detail_x, coarse_x, payload = pl.pallas_call(
        functools.partial(first_kernel, count=n_gx),
        grid=(chunks,),
        in_specs=[
            pl.BlockSpec((length, rows, depth), lambda i: (0, i, 0)),
            pl.BlockSpec((3, rows, depth), lambda i: (0, i, 0)),
            pl.BlockSpec((8, 128), lambda i: (0, 0)),
            smem,
            pl.BlockSpec((8, width), lambda i: (0, 0)),
            pl.BlockSpec((width, width), lambda i: (0, 0)),
            pl.BlockSpec((1, width), lambda i: (0, 0)),
        ],
        out_specs=[
            pl.BlockSpec((half, rows, depth), lambda i: (0, i, 0)),
            pl.BlockSpec((half, rows, depth), lambda i: (0, i, 0)),
            pl.BlockSpec((1, 8, half * rows), lambda i: (i, 0, 0)),
        ],
        out_shape=[
            jax.ShapeDtypeStruct((half, lines, depth), jnp.float32),
            jax.ShapeDtypeStruct((half, lines, depth), jnp.float32),
            jax.ShapeDtypeStruct((chunks, 8, half * rows), jnp.float32),
        ],
        scratch_shapes=[pltpu.VMEM((8, depth), jnp.float32)],
        compiler_params=params,
        name="pass_first",
    )(nodes, planes, most, scalars, coefz, factor_z, gain_row)

    gathered = lax.all_gather(payload, "gz")

    held = group * capacity + (room + 1 if listed else 1)
    detail_z, outgoing, level = pl.pallas_call(
        functools.partial(
            third_kernel, count=n_gz, chunks=chunks, levels=levels, head=group * capacity
        ),
        grid=(chunks,),
        in_specs=[
            smem,
            pl.BlockSpec((half, rows, depth), lambda i: (0, i, 0)),
            pl.BlockSpec((n_gz, 1, 8, half * rows), lambda i: (0, i, 0, 0)),
            pl.BlockSpec((8, width), lambda i: (0, 0)),
            pl.BlockSpec((width, width), lambda i: (0, 0)),
            pl.BlockSpec((1, width), lambda i: (0, 0)),
            pl.BlockSpec((2 * LINES, width), lambda i: (0, 0)),
        ],
        out_specs=[
            pl.BlockSpec((half, rows, width), lambda i: (0, i, 0)),
            pl.BlockSpec((held, 2 * LINES, width), lambda i: (0, 0, 0)),
            smem,
        ],
        out_shape=[
            jax.ShapeDtypeStruct((half, lines, width), jnp.float32),
            jax.ShapeDtypeStruct((held, 2 * LINES, width), jnp.float32),
            jax.ShapeDtypeStruct((1,), jnp.int32),
        ],
        scratch_shapes=[
            pltpu.VMEM((depth, depth), jnp.float32),
            pltpu.VMEM((8, depth), jnp.float32),
            pltpu.VMEM((2, half * rows // 8, 8, width), jnp.float32),
        ],
        compiler_params=params,
        name="pass_third",
    )(placed, coarse_x, gathered, coefz, factor_z, gain_row, header)

    if listed:
        received = spread(outgoing, group, room, levels, level[0])
    else:
        outgoing = outgoing[: group * capacity].reshape(group, capacity, 2 * LINES, width)
        received = pl.pallas_call(
            functools.partial(deliver_kernel, n_gy, n_gz),
            out_shape=jax.ShapeDtypeStruct(outgoing.shape, jnp.float32),
            in_specs=[hbm],
            out_specs=hbm,
            scratch_shapes=[
                pltpu.SemaphoreType.DMA((group - 1,)),
                pltpu.SemaphoreType.DMA((group - 1,)),
                pltpu.SemaphoreType.DMA,
            ],
            compiler_params=pltpu.CompilerParams(collective_id=1, has_side_effects=True),
            name="deliver",
        )(outgoing)
    return (
        detail_x,
        detail_z,
        received.reshape(1, group, capacity, 2, LINES, width),
    )


def solution(mesh):
    sizes = tuple(mesh.shape[axis] for axis in ("gx", "gy", "gz"))
    return jax.shard_map(
        functools.partial(local, sizes),
        mesh=mesh,
        in_specs=(
            P("gx", "gy", "gz"),
            P(),
            P(),
            P("gx", None),
            P("gx"),
            P("gz", None),
            P("gz"),
            P(("gx", "gy", "gz"), None),
        ),
        out_specs=(
            P("gx", "gy", "gz"),
            P("gx", "gy", "gz"),
            P(("gx", "gy", "gz"), None, None, None, None, None),
        ),
        check_vma=False,
    )
```

```python
import functools

import jax
import jax.numpy as jnp
from jax import lax
from jax.experimental import pallas as pl
from jax.experimental.pallas import tpu as pltpu
from jax.sharding import PartitionSpec as P

LINES = 4
MESH = pl.DeviceIdType.MESH
HIGHEST = lax.Precision.HIGHEST
LIMIT = 56 * 1024 * 1024


def neighbours(spacing):
    count = spacing.shape[1]
    parts, rest = [], spacing
    for _ in range(3):
        part = rest.astype(jnp.bfloat16).astype(jnp.float32)
        parts.append(part)
        rest = rest - part
    kind = lax.broadcasted_iota(jnp.int32, (16, count), 0)
    stacked = jnp.zeros((16, count), jnp.float32)
    for k, part in enumerate(parts):
        stacked = jnp.where(kind == k, part, stacked)
    row = lax.broadcasted_iota(jnp.int32, (count, 128), 0)
    twice = 2 * lax.broadcasted_iota(jnp.int32, (count, 128), 1)
    chosen = [
        jnp.dot(
            stacked.astype(jnp.bfloat16),
            jnp.where(row == twice + shift, 1.0, 0.0).astype(jnp.bfloat16),
            preferred_element_type=jnp.float32,
        )
        for shift in (0, 1, -2, -1)
    ]
    return [jnp.sum(one, axis=0, keepdims=True) for one in chosen]


def coefficients(even, odd, even_before, odd_before):
    def parts(even, odd):
        total = even + odd
        total = jnp.where(total > 0, total, 1.0)
        return odd / total, even / total

    return (
        parts(even, odd) + (0.5 * even, 0.5 * odd_before) + parts(even_before, odd_before)
    )


def prepare_kernel(
    spacing_x, spacing_z, factor, gain, targets, scalars, coefz, placed, header, *, group,
    capacity, listed,
):
    half = factor.shape[0]
    scalars[...] = jnp.zeros_like(scalars)
    for k, row in enumerate(coefficients(*neighbours(spacing_x[...]))):
        scalars[k : k + 1, :] = row
    scalars[8 : 8 + half, 0:half] = factor[...]
    scalars[8 + half : 9 + half, 0:half] = gain[...]

    me = lax.axis_index("gz")
    width = coefz.shape[1]
    start = pl.multiple_of(me * (2 * width), 2 * width)
    here = neighbours(spacing_z[:, pl.ds(start, 2 * width)])
    earlier = pl.multiple_of(jnp.maximum(start - width, 0), width)
    previous = spacing_z[:, pl.ds(earlier, width)]
    lane = lax.broadcasted_iota(jnp.int32, (1, width), 1)
    inside = jnp.where(me > 0, 1.0, 0.0)
    first = lane == 0
    even_before = jnp.where(first, inside * previous[:, width - 2 : width - 1], here[2])
    odd_before = jnp.where(first, inside * previous[:, width - 1 : width], here[3])
    coefz[...] = jnp.zeros_like(coefz)
    for k, row in enumerate(coefficients(here[0], here[1], even_before, odd_before)):
        coefz[k : k + 1, :] = row

    blocks = targets.shape[1]
    member = lax.broadcasted_iota(jnp.int32, (group, blocks), 0)
    named = jnp.where(member == targets[...], 1.0, 0.0)
    before = lax.broadcasted_iota(jnp.int32, (blocks, blocks), 0)
    after = lax.broadcasted_iota(jnp.int32, (blocks, blocks), 1)
    counted = jnp.dot(
        named.astype(jnp.bfloat16),
        jnp.where(before < after, 1.0, 0.0).astype(jnp.bfloat16),
        preferred_element_type=jnp.float32,
    )
    slot = jnp.sum(named * counted, axis=0, keepdims=True).astype(jnp.int32)
    place = targets[...] * capacity + slot
    header[...] = jnp.zeros_like(header)
    if listed:
        direct = capacity // 2
        there = 1 - lax.axis_index("gy") // 2
        tally = jnp.sum(named, axis=1, keepdims=True)
        kind = lax.broadcasted_iota(jnp.int32, (group, 1), 0)
        more = jnp.where(kind // 4 == there, jnp.maximum(tally - direct, 0.0), 0.0)
        ahead = jnp.sum(jnp.where(member < targets[...], more, 0.0), axis=0, keepdims=True)
        listing = group * capacity + 1 - direct + ahead.astype(jnp.int32) + slot
        place = jnp.where((targets[...] // 4 == there) & (slot >= direct), listing, place)
        side = lax.broadcasted_iota(jnp.int32, (group, 128), 0)
        across = lax.broadcasted_iota(jnp.int32, (group, 128), 1)
        header[0:1, :] = jnp.sum(jnp.where(side == across, more, 0.0), axis=0, keepdims=True)
        scalars[9 + half : 10 + half, :] = jnp.sum(more, axis=0, keepdims=True) + jnp.zeros(
            (1, 128), jnp.float32
        )
    placed[...] = place


class Table:
    def __init__(self, scalars):
        self.scalars = scalars

    def __getitem__(self, place):
        return self.scalars[8 + place[0], place[1]]


def exchange_first(
    count, over, scalars, hbm_nodes, out, most, nodes, left, right, send, tails, needs, wants,
    send_sem, recv_sem, need_send, need_recv, want_send, want_recv, load_sem,
):
    me, row = lax.axis_index("gx"), lax.axis_index("gy")
    load = pltpu.make_async_copy(hbm_nodes, nodes, load_sem)
    load.start()
    half = nodes.shape[0] // 2
    lines = nodes.shape[1]
    barrier = pltpu.get_barrier_semaphore()
    for d in range(1, count):
        pl.semaphore_signal(
            barrier, inc=1, device_id={"gx": lax.rem(me + d, count)}, device_id_type=MESH
        )
    for d in range(1, over):
        pl.semaphore_signal(
            barrier, inc=1, device_id={"gy": lax.rem(row + d, over)}, device_id_type=MESH
        )

    def coef(kind, k):
        return scalars[kind, me * half + k]

    factor = Table(scalars)
    gain_last = scalars[8 + half, half - 1]
    needs[0] = jnp.full(needs.shape[1:], scalars[9 + half, 0], jnp.float32)
    load.wait()

    last = half - 1
    send[1, pl.ds(0, lines), :] = nodes[2 * last + 1] - coef(0, last) * nodes[2 * last]
    pl.semaphore_wait(barrier, count + over - 2)

    to_right = pltpu.make_async_remote_copy(
        src_ref=send.at[1, pl.ds(0, lines)], dst_ref=left, send_sem=send_sem.at[0], recv_sem=recv_sem.at[0],
        device_id={"gx": lax.rem(me + 1, count)}, device_id_type=MESH,
    )
    to_left = pltpu.make_async_remote_copy(
        src_ref=nodes.at[0], dst_ref=right, send_sem=send_sem.at[1], recv_sem=recv_sem.at[1],
        device_id={"gx": lax.rem(me + count - 1, count)}, device_id_type=MESH,
    )

    @pl.when(me < count - 1)
    def _():
        to_right.start()

    @pl.when(me > 0)
    def _():
        to_left.start()

    small = []
    for d in range(1, count):
        small.append(
            pltpu.make_async_remote_copy(
                src_ref=needs.at[0], dst_ref=needs.at[d],
                send_sem=need_send.at[d], recv_sem=need_recv.at[d],
                device_id={"gx": lax.rem(me + d, count)}, device_id_type=MESH,
            )
        )
        small[-1].start()

    weights = []
    for k in range(half):
        weight = factor[last, k] * coef(2, k)
        if k < last:
            weight = weight + factor[last, k + 1] * coef(3, k + 1)
        weights.append(weight)
    edge = factor[last, 0] * coef(3, 0)

    def chunk(i, carry):
        rows = pl.ds(pl.multiple_of(i * 8, 8), 8)
        even = nodes[0, rows, :]
        value = (-edge * coef(5, 0)) * even
        for k in range(half):
            detail = nodes[2 * k + 1, rows, :] - coef(0, k) * even
            if k < last:
                even = nodes[2 * k + 2, rows, :]
                detail = detail - coef(1, k) * even
            value = value + weights[k] * detail
        send[0, rows, :] = value
        return carry

    lax.fori_loop(0, lines // 8, chunk, 0)
    for one in small:
        one.wait_recv()
    wants[0] = jnp.max(needs[...], axis=0)
    for d in range(1, over):
        small.append(
            pltpu.make_async_remote_copy(
                src_ref=wants.at[0], dst_ref=wants.at[d],
                send_sem=want_send.at[d], recv_sem=want_recv.at[d],
                device_id={"gy": lax.rem(row + d, over)}, device_id_type=MESH,
            )
        )
        small[-1].start()

    @pl.when(me == 0)
    def _():
        left[...] = jnp.zeros_like(left)

    @pl.when(me == count - 1)
    def _():
        right[...] = jnp.zeros_like(right)

    @pl.when(me > 0)
    def _():
        to_right.wait_recv()

    @pl.when(me < count - 1)
    def _():
        to_left.wait_recv()

    end = -(factor[last, last] * coef(2, last)) * coef(1, last)
    own = send.at[0]
    own[pl.ds(0, lines), :] = own[pl.ds(0, lines), :] + edge * left[...] + end * right[...]
    own[pl.ds(lines, 8), :] = jnp.full((8, own.shape[1]), gain_last, jnp.float32)

    copies = []
    for d in range(1, count):
        copies.append(
            pltpu.make_async_remote_copy(
                src_ref=tails.at[0], dst_ref=tails.at[d],
                send_sem=send_sem.at[1 + d], recv_sem=recv_sem.at[1 + d],
                device_id={"gx": lax.rem(me + d, count)}, device_id_type=MESH,
            )
        )
    tails[0] = own[...]
    for d in range(1, count):

        @pl.when(me + d < count)
        def _(d=d):
            copies[d - 1].start()

    out[0] = left[...]
    out[1] = right[...]
    out[2] = jnp.zeros_like(left)
    for d in range(count - 1, 0, -1):

        @pl.when(me >= d)
        def _(d=d):
            copies[d - 1].wait_recv()
            out[2] = (
                tails[d, pl.ds(0, lines), :]
                + jnp.max(tails[d, pl.ds(lines, 8), :], axis=0, keepdims=True) * out[2]
            )

    for one in small[count - 1 :]:
        one.wait_recv()
    most[...] = jnp.max(wants[...], axis=0)
    for one in small:
        one.wait_send()

    @pl.when(me < count - 1)
    def _():
        to_right.wait_send()

    @pl.when(me > 0)
    def _():
        to_left.wait_send()

    for d in range(1, count):

        @pl.when(me + d < count)
        def _(d=d):
            copies[d - 1].wait_send()


def loads(coefz):
    width = coefz.shape[1]
    row = lax.broadcasted_iota(jnp.int32, (2 * width, width), 0)
    twice = 2 * lax.broadcasted_iota(jnp.int32, (2 * width, width), 1)
    a, b, half_even, half_odd, a_before, b_before = [coefz[k : k + 1, :] for k in range(6)]
    zero = jnp.zeros((2 * width, width), jnp.float32)
    detail = jnp.where(row == twice, -a, zero)
    detail = jnp.where(row == twice + 1, 1.0, detail)
    detail = jnp.where(row == twice + 2, -b, detail)
    earlier = jnp.where(row == twice - 2, -a_before, zero)
    earlier = jnp.where(row == twice - 1, 1.0, earlier)
    earlier = jnp.where(row == twice, -b_before, earlier)
    return detail, half_even * detail + half_odd * earlier, row == twice


def first_kernel(
    nodes, planes, most, scalars, coefz, factor_z, gain_z, detail, coarse, payload, weights,
    *, count,
):
    me = lax.axis_index("gx")
    half = detail.shape[0]
    factor = Table(scalars)

    def coef(row, k):
        return scalars[row, me * half + k]

    width = factor_z.shape[0]

    @pl.when(pl.program_id(0) == 0)
    def _():
        load = loads(coefz)[1]
        tail = lax.dot_general(
            factor_z[pl.ds(width - 8, 8), :], load, (((1,), (1,)), ((), ())), precision=HIGHEST
        )
        lane = lax.broadcasted_iota(jnp.int32, (1, 2 * width), 1)
        a_last = coefz[0:1, width - 1 : width]
        weights[...] = jnp.zeros_like(weights)
        weights[0:1, :] = jnp.where(lane == 0, 1.0, 0.0)
        weights[1:2, :] = jnp.where(
            lane == 2 * width - 2, -a_last, jnp.where(lane == 2 * width - 1, 1.0, 0.0)
        )
        weights[2:3, :] = tail[7:8, :]

    for i in range(nodes.shape[1] // 8):
        rows = pl.ds(i * 8, 8)
        even = [nodes[2 * k, rows, :] for k in range(half)]
        before = planes[0, rows, :] - coef(5, 0) * even[0]
        load = []
        for k in range(half):
            after = even[k + 1] if k + 1 < half else planes[1, rows, :]
            value = nodes[2 * k + 1, rows, :] - coef(0, k) * even[k] - coef(1, k) * after
            detail[k, rows, :] = value
            load.append(coef(2, k) * value + coef(3, k) * before)
            before = value
        for k in range(half):
            value = nodes[2 * k, rows, :] + scalars[8 + half, k] * planes[2, rows, :]
            for j in range(half):
                value = value + factor[k, j] * load[j]
            coarse[k, rows, :] = value

    lines = coarse[...].reshape(half * coarse.shape[1], coarse.shape[2])
    sent = lax.dot_general(
        weights[...], lines, (((1,), (1,)), ((), ())), precision=HIGHEST
    )
    kind = lax.broadcasted_iota(jnp.int32, sent.shape, 0)
    end_gain = gain_z[0:1, width - 1 : width]
    end_first = factor_z[width - 1 : width, 0:1] * coefz[3:4, 0:1]
    end_last = -(
        factor_z[width - 1 : width, width - 1 : width]
        * coefz[2:3, width - 1 : width]
        * coefz[1:2, width - 1 : width]
    )
    sent = jnp.where(kind == 3, end_gain, sent)
    sent = jnp.where(kind == 4, end_first, sent)
    sent = jnp.where(kind == 5, end_last, sent)
    sent = jnp.where(kind == 6, most[0:1, 0:1], sent)
    payload[0] = sent


def third_kernel(
    placed, coarse, gathered, coefz, factor_z, gain_z, header, detail, outgoing, level, matrix,
    update, tiles, *, count, chunks, levels, head,
):
    me = lax.axis_index("gz")
    step = pl.program_id(0)
    width = factor_z.shape[0]

    @pl.when(step == 0)
    def _():
        outgoing[...] = jnp.zeros_like(outgoing)
        outgoing[head] = header[...]
        need = jnp.max(gathered[:, 0, 6:7, :])
        level[0] = sum((need > sent).astype(jnp.int32) for sent in levels)
        detail_of, load_of, is_even = loads(coefz)
        solved = lax.dot_general(
            load_of, factor_z[...], (((1,), (1,)), ((), ())), precision=HIGHEST
        )
        matrix[:, 0:width] = jnp.where(is_even, 1.0, 0.0) + solved
        matrix[:, width:] = detail_of
        turned = factor_z[...].T
        b_last = coefz[1:2, width - 1 : width]
        lane = lax.broadcasted_iota(jnp.int32, (1, width), 1)
        update[...] = jnp.zeros_like(update)
        update[0:1, 0:width] = -turned[width - 1 : width, :] * (
            coefz[2:3, width - 1 : width] * b_last
        )
        update[0:1, width:] = jnp.where(lane == width - 1, -b_last, 0.0)
        update[1:2, 0:width] = turned[0:1, :] * coefz[3:4, 0:1]
        update[2:3, 0:width] = gain_z[...]

    def heard(p, row):
        return gathered[p, 0, row : row + 1, :]

    empty = jnp.zeros_like(heard(0, 0))
    right, left, carry = empty, empty, empty
    for p in range(count):
        right = jnp.where(me + 1 == p, heard(p, 0), right)
        left = jnp.where(me - 1 == p, heard(p, 1), left)
        if p < count - 1:
            tail = heard(p, 2) + heard(p, 5) * heard(p + 1, 0) + heard(p, 3) * carry
            if p > 0:
                tail = tail + heard(p, 4) * heard(p - 1, 1)
            carry = jnp.where(p < me, tail, carry)
    kind = lax.broadcasted_iota(jnp.int32, (8, empty.shape[1]), 0)
    edges = jnp.where(kind == 0, right, jnp.where(kind == 1, left, jnp.where(kind == 2, carry, 0.0)))

    rows = coarse.shape[0] * coarse.shape[1]
    lines = coarse[...].reshape(rows, coarse.shape[2])
    result = jnp.dot(lines, matrix[...], precision=HIGHEST) + lax.dot_general(
        edges, update[...], (((0,), (0,)), ((), ())), precision=HIGHEST
    )
    upper = result[:, :width].reshape(rows // 8, 8, width)
    lower = result[:, width:].reshape(rows // 8, 8, width)
    detail[...] = result[:, width:].reshape(detail.shape)
    top = lax.broadcasted_iota(jnp.int32, upper.shape, 1) < LINES
    tiles[0] = jnp.where(top, upper, pltpu.roll(lower, LINES, 1))
    tiles[1] = jnp.where(top, pltpu.roll(upper, LINES, 1), lower)
    eights = coarse.shape[1] // 8

    def scatter(x, carry):
        for j in range(eights):
            for half in range(2):
                block = x * (2 * eights * chunks) + step * (2 * eights) + 2 * j + half
                outgoing[placed[0, block]] = tiles[half, x * eights + j]
        return carry

    lax.fori_loop(0, coarse.shape[0], scatter, 0)


def deliver_kernel(n_gy, n_gz, outgoing, received, send_sem, recv_sem, own_sem):
    gy, gz = lax.axis_index("gy"), lax.axis_index("gz")
    me = gy * n_gz + gz
    shifts = [
        (dy, dz) for dy in range(n_gy) for dz in range(n_gz) if dy + dz > 0
    ]
    shifts.sort(key=lambda shift: -min(shift[0], n_gy - shift[0]))
    barrier = pltpu.get_barrier_semaphore()
    targets = []
    for dy, dz in shifts:
        there = (lax.rem(gy + dy, n_gy), lax.rem(gz + dz, n_gz))
        targets.append(there)
        pl.semaphore_signal(
            barrier, inc=1, device_id={"gy": there[0], "gz": there[1]}, device_id_type=MESH
        )
    own = pltpu.make_async_copy(outgoing.at[me], received.at[me], own_sem)
    own.start()
    pl.semaphore_wait(barrier, len(shifts))
    copies = []
    for k, there in enumerate(targets):
        copy = pltpu.make_async_remote_copy(
            src_ref=outgoing.at[there[0] * n_gz + there[1]],
            dst_ref=received.at[me],
            send_sem=send_sem.at[k],
            recv_sem=recv_sem.at[k],
            device_id={"gy": there[0], "gz": there[1]},
            device_id_type=MESH,
        )
        copy.start()
        copies.append(copy)
    own.wait()
    for copy in copies:
        copy.wait()


def spread_kernel(sent, outgoing, received, lists, send_sem, recv_sem, own_sem):
    gy, gz = lax.axis_index("gy"), lax.axis_index("gz")
    half, place = gy // 2, lax.rem(gy, 2)
    me = gy * 2 + gz
    capacity = received.shape[1]

    def at(step):
        h, y, z = step
        there_half = 1 - half if h else half
        there_place = 1 - place if y else place
        return there_half * 2 + there_place, 1 - gz if z else gz

    steps = [(h, y, z) for h in (0, 1) for y in (0, 1) for z in (0, 1) if h + y + z]
    barrier = pltpu.get_barrier_semaphore()
    for step in steps:
        there = at(step)
        pl.semaphore_signal(
            barrier, inc=1, device_id={"gy": there[0], "gz": there[1]}, device_id_type=MESH
        )
    own = pltpu.make_async_copy(
        outgoing.at[pl.ds(me * capacity, capacity)], received.at[me], own_sem
    )
    own.start()
    pl.semaphore_wait(barrier, len(steps))

    def copy(k, step, source, target):
        there = at(step)
        return pltpu.make_async_remote_copy(
            src_ref=source, dst_ref=target, send_sem=send_sem.at[k], recv_sem=recv_sem.at[k],
            device_id={"gy": there[0], "gz": there[1]}, device_id_type=MESH,
        )

    def direct(step):
        there = at(step)
        count = capacity // 2 if step[0] else capacity
        return copy(
            steps.index(step), step,
            outgoing.at[pl.ds((there[0] * 2 + there[1]) * capacity, count)],
            received.at[me, pl.ds(0, count)],
        )

    mine, beside = place * 2 + gz, (1 - place) * 2 + gz
    rows = pl.ds(0, 1 + sent)
    tail = pl.ds(received.shape[0] * capacity, 1 + sent)
    across = copy(7, (1, 0, 0), outgoing.at[tail], lists.at[mine, rows])
    along = copy(8, (0, 1, 0), lists.at[mine, rows], lists.at[mine, rows])
    to_core = copy(9, (0, 0, 1), lists.at[mine, rows], lists.at[mine, rows])
    to_core_too = copy(10, (0, 0, 1), lists.at[beside, rows], lists.at[beside, rows])
    early = [direct((0, 1, 0)), direct((0, 0, 1))]
    late = [direct(step) for step in ((1, 0, 0), (1, 0, 1), (1, 1, 0), (1, 1, 1), (0, 1, 1))]
    across.start()
    for one in early:
        one.start()
    across.wait_recv()
    along.start()
    to_core.start()
    for one in late:
        one.start()
    along.wait_recv()
    to_core_too.start()
    own.wait()
    across.wait_send()
    along.wait_send()
    for one in early + late + [to_core, to_core_too]:
        one.wait()


def gather_kernel(sent, base, hbm_lists, received, lists, tiles, sems):
    direct = tiles.shape[1]
    half = lax.axis_index("gy") // 2
    me = lax.axis_index("gy") * 2 + lax.axis_index("gz")
    rows = pl.ds(0, 1 + sent)
    loads = [
        pltpu.make_async_copy(hbm_lists.at[k, rows], lists.at[k, rows], sems.at[0, k])
        for k in range(4)
    ]
    for one in loads:
        one.start()
    whole, stores = [], []
    for k in range(4):
        near, far = half * 4 + k, (1 - half) * 4 + k
        whole.append(pltpu.make_async_copy(base.at[near], received.at[near], sems.at[1, k]))
        whole.append(
            pltpu.make_async_copy(
                base.at[far, pl.ds(0, direct)], received.at[far, pl.ds(0, direct)], sems.at[2, k]
            )
        )
        stores.append(
            pltpu.make_async_copy(
                tiles.at[k], received.at[far, pl.ds(direct, direct)], sems.at[3, k]
            )
        )
    for one in whole:
        one.start()
    for k in range(4):
        loads[k].wait()
        header = lists[k, 0, 0:1, :]
        lane = lax.broadcasted_iota(jnp.int32, header.shape, 1)
        start = jnp.sum(jnp.where((lane >= half * 4) & (lane < me), header, 0.0))
        count = jnp.sum(jnp.where(lane == me, header, 0.0)).astype(jnp.int32)
        listed = lists[k, pl.ds(1 + start.astype(jnp.int32), direct)]
        slot = lax.broadcasted_iota(jnp.int32, listed.shape, 0)
        tiles[k] = jnp.where(slot < count, listed, 0.0)
        stores[k].start()
    for one in whole + stores:
        one.wait()


def spread(outgoing, group, room, levels, level):
    capacity = (outgoing.shape[0] - room - 1) // group
    tile = outgoing.shape[1:]
    direct = capacity // 2

    def branch(number, sent):
        def run(outgoing):
            base, lists = pl.pallas_call(
                functools.partial(spread_kernel, sent),
                out_shape=[
                    jax.ShapeDtypeStruct((group, capacity) + tile, jnp.float32),
                    jax.ShapeDtypeStruct((group // 2, room + 1) + tile, jnp.float32),
                ],
                in_specs=[pl.BlockSpec(memory_space=pl.ANY)],
                out_specs=[pl.BlockSpec(memory_space=pl.ANY)] * 2,
                scratch_shapes=[
                    pltpu.SemaphoreType.DMA((11,)),
                    pltpu.SemaphoreType.DMA((11,)),
                    pltpu.SemaphoreType.DMA,
                ],
                compiler_params=pltpu.CompilerParams(
                    collective_id=2 + number, has_side_effects=True
                ),
                name="spread",
            )(outgoing)
            return pl.pallas_call(
                functools.partial(gather_kernel, sent),
                in_specs=[pl.BlockSpec(memory_space=pl.ANY)] * 2,
                out_specs=pl.BlockSpec(memory_space=pltpu.HBM),
                scratch_shapes=[
                    pltpu.VMEM((group // 2, room + 1) + tile, jnp.float32),
                    pltpu.VMEM((group // 2, direct) + tile, jnp.float32),
                    pltpu.SemaphoreType.DMA((4, group // 2)),
                ],
                out_shape=jax.ShapeDtypeStruct(base.shape, jnp.float32),
                compiler_params=pltpu.CompilerParams(vmem_limit_bytes=LIMIT),
                name="gather",
            )(base, lists)

        return run

    branches = [branch(k, sent) for k, sent in enumerate(levels + (room,))]
    return lax.switch(level, branches, outgoing)


def local(sizes, nodes, spacing_x, spacing_z, factor_x, gain_x, factor_z, gain_z, receivers):
    n_gx, n_gy, n_gz = sizes
    length, lines, depth = nodes.shape
    half, width = length // 2, depth // 2
    group = n_gy * n_gz
    blocks = half * lines // LINES
    capacity = max(2, blocks // group * 2)
    listed = n_gy == 4 and n_gz == 2
    direct = capacity // 2
    room = group // 2 * (capacity - direct) if listed else 0
    levels = tuple(room * k // 16 for k in range(5, 11))
    scalars, coefz, placed, header = pl.pallas_call(
        functools.partial(prepare_kernel, group=group, capacity=capacity, listed=listed),
        out_shape=[
            jax.ShapeDtypeStruct((32, 128), jnp.float32),
            jax.ShapeDtypeStruct((8, width), jnp.float32),
            jax.ShapeDtypeStruct((1, blocks), jnp.int32),
            jax.ShapeDtypeStruct((2 * LINES, 128), jnp.float32),
        ],
        compiler_params=pltpu.CompilerParams(vmem_limit_bytes=LIMIT),
        name="prepare",
    )(
        spacing_x.reshape(1, -1), spacing_z.reshape(1, -1), factor_x, gain_x.reshape(1, -1),
        receivers.reshape(1, -1),
    )
    gain_row = gain_z.reshape(1, width)
    vmem = pl.BlockSpec(memory_space=pltpu.VMEM)
    smem = pl.BlockSpec(memory_space=pltpu.SMEM)
    hbm = pl.BlockSpec(memory_space=pl.ANY)

    planes, most = pl.pallas_call(
        functools.partial(exchange_first, n_gx, n_gy),
        out_shape=[
            jax.ShapeDtypeStruct((3, lines, depth), jnp.float32),
            jax.ShapeDtypeStruct((8, 128), jnp.float32),
        ],
        in_specs=[smem, hbm],
        out_specs=[vmem, vmem],
        scratch_shapes=[
            pltpu.VMEM((length, lines, depth), jnp.float32),
            pltpu.VMEM((lines, depth), jnp.float32),
            pltpu.VMEM((lines, depth), jnp.float32),
            pltpu.VMEM((2, lines + 8, depth), jnp.float32),
            pltpu.VMEM((n_gx, lines + 8, depth), jnp.float32),
            pltpu.VMEM((n_gx, 8, 128), jnp.float32),
            pltpu.VMEM((n_gy, 8, 128), jnp.float32),
            pltpu.SemaphoreType.DMA((n_gx + 1,)),
            pltpu.SemaphoreType.DMA((n_gx + 1,)),
            pltpu.SemaphoreType.DMA((n_gx,)),
            pltpu.SemaphoreType.DMA((n_gx,)),
            pltpu.SemaphoreType.DMA((n_gy,)),
            pltpu.SemaphoreType.DMA((n_gy,)),
            pltpu.SemaphoreType.DMA,
        ],
        compiler_params=pltpu.CompilerParams(
            collective_id=0, has_side_effects=True, vmem_limit_bytes=LIMIT
        ),
        name="exchange_first",
    )(scalars, nodes)

    chunks = 4
    rows = lines // chunks
    params = pltpu.CompilerParams(
        dimension_semantics=("arbitrary",), vmem_limit_bytes=LIMIT
    )
    detail_x, coarse_x, payload = pl.pallas_call(
        functools.partial(first_kernel, count=n_gx),
        grid=(chunks,),
        in_specs=[
            pl.BlockSpec((length, rows, depth), lambda i: (0, i, 0)),
            pl.BlockSpec((3, rows, depth), lambda i: (0, i, 0)),
            pl.BlockSpec((8, 128), lambda i: (0, 0)),
            smem,
            pl.BlockSpec((8, width), lambda i: (0, 0)),
            pl.BlockSpec((width, width), lambda i: (0, 0)),
            pl.BlockSpec((1, width), lambda i: (0, 0)),
        ],
        out_specs=[
            pl.BlockSpec((half, rows, depth), lambda i: (0, i, 0)),
            pl.BlockSpec((half, rows, depth), lambda i: (0, i, 0)),
            pl.BlockSpec((1, 8, half * rows), lambda i: (i, 0, 0)),
        ],
        out_shape=[
            jax.ShapeDtypeStruct((half, lines, depth), jnp.float32),
            jax.ShapeDtypeStruct((half, lines, depth), jnp.float32),
            jax.ShapeDtypeStruct((chunks, 8, half * rows), jnp.float32),
        ],
        scratch_shapes=[pltpu.VMEM((8, depth), jnp.float32)],
        compiler_params=params,
        name="pass_first",
    )(nodes, planes, most, scalars, coefz, factor_z, gain_row)

    gathered = lax.all_gather(payload, "gz")

    held = group * capacity + (room + 1 if listed else 1)
    detail_z, outgoing, level = pl.pallas_call(
        functools.partial(
            third_kernel, count=n_gz, chunks=chunks, levels=levels, head=group * capacity
        ),
        grid=(chunks,),
        in_specs=[
            smem,
            pl.BlockSpec((half, rows, depth), lambda i: (0, i, 0)),
            pl.BlockSpec((n_gz, 1, 8, half * rows), lambda i: (0, i, 0, 0)),
            pl.BlockSpec((8, width), lambda i: (0, 0)),
            pl.BlockSpec((width, width), lambda i: (0, 0)),
            pl.BlockSpec((1, width), lambda i: (0, 0)),
            pl.BlockSpec((2 * LINES, width), lambda i: (0, 0)),
        ],
        out_specs=[
            pl.BlockSpec((half, rows, width), lambda i: (0, i, 0)),
            pl.BlockSpec((held, 2 * LINES, width), lambda i: (0, 0, 0)),
            smem,
        ],
        out_shape=[
            jax.ShapeDtypeStruct((half, lines, width), jnp.float32),
            jax.ShapeDtypeStruct((held, 2 * LINES, width), jnp.float32),
            jax.ShapeDtypeStruct((1,), jnp.int32),
        ],
        scratch_shapes=[
            pltpu.VMEM((depth, depth), jnp.float32),
            pltpu.VMEM((8, depth), jnp.float32),
            pltpu.VMEM((2, half * rows // 8, 8, width), jnp.float32),
        ],
        compiler_params=params,
        name="pass_third",
    )(placed, coarse_x, gathered, coefz, factor_z, gain_row, header)

    if listed:
        received = spread(outgoing, group, room, levels, level[0])
    else:
        outgoing = outgoing[: group * capacity].reshape(group, capacity, 2 * LINES, width)
        received = pl.pallas_call(
            functools.partial(deliver_kernel, n_gy, n_gz),
            out_shape=jax.ShapeDtypeStruct(outgoing.shape, jnp.float32),
            in_specs=[hbm],
            out_specs=hbm,
            scratch_shapes=[
                pltpu.SemaphoreType.DMA((group - 1,)),
                pltpu.SemaphoreType.DMA((group - 1,)),
                pltpu.SemaphoreType.DMA,
            ],
            compiler_params=pltpu.CompilerParams(collective_id=1, has_side_effects=True),
            name="deliver",
        )(outgoing)
    return (
        detail_x,
        detail_z,
        received.reshape(1, group, capacity, 2, LINES, width),
    )


def solution(mesh):
    sizes = tuple(mesh.shape[axis] for axis in ("gx", "gy", "gz"))
    return jax.shard_map(
        functools.partial(local, sizes),
        mesh=mesh,
        in_specs=(
            P("gx", "gy", "gz"),
            P(),
            P(),
            P("gx", None),
            P("gx"),
            P("gz", None),
            P("gz"),
            P(("gx", "gy", "gz"), None),
        ),
        out_specs=(
            P("gx", "gy", "gz"),
            P("gx", "gy", "gz"),
            P(("gx", "gy", "gz"), None, None, None, None, None),
        ),
        check_vma=False,
    )
```

```python
import functools

import jax
import jax.numpy as jnp
from jax import lax
from jax.experimental import pallas as pl
from jax.experimental.pallas import tpu as pltpu
from jax.sharding import PartitionSpec as P

LINES = 4
MESH = pl.DeviceIdType.MESH
HIGHEST = lax.Precision.HIGHEST
LIMIT = 56 * 1024 * 1024


def neighbours(spacing):
    count = spacing.shape[1]
    parts, rest = [], spacing
    for _ in range(3):
        part = rest.astype(jnp.bfloat16).astype(jnp.float32)
        parts.append(part)
        rest = rest - part
    kind = lax.broadcasted_iota(jnp.int32, (16, count), 0)
    stacked = jnp.zeros((16, count), jnp.float32)
    for k, part in enumerate(parts):
        stacked = jnp.where(kind == k, part, stacked)
    row = lax.broadcasted_iota(jnp.int32, (count, 128), 0)
    twice = 2 * lax.broadcasted_iota(jnp.int32, (count, 128), 1)
    chosen = [
        jnp.dot(
            stacked.astype(jnp.bfloat16),
            jnp.where(row == twice + shift, 1.0, 0.0).astype(jnp.bfloat16),
            preferred_element_type=jnp.float32,
        )
        for shift in (0, 1, -2, -1)
    ]
    return [jnp.sum(one, axis=0, keepdims=True) for one in chosen]


def coefficients(even, odd, even_before, odd_before):
    def parts(even, odd):
        total = even + odd
        total = jnp.where(total > 0, total, 1.0)
        return odd / total, even / total

    return (
        parts(even, odd) + (0.5 * even, 0.5 * odd_before) + parts(even_before, odd_before)
    )


def prepare_kernel(
    spacing_x, spacing_z, factor, gain, targets, scalars, coefz, placed, header, *, group,
    capacity, listed,
):
    half = factor.shape[0]
    scalars[...] = jnp.zeros_like(scalars)
    for k, row in enumerate(coefficients(*neighbours(spacing_x[...]))):
        scalars[k : k + 1, :] = row
    scalars[8 : 8 + half, 0:half] = factor[...]
    scalars[8 + half : 9 + half, 0:half] = gain[...]

    me = lax.axis_index("gz")
    width = coefz.shape[1]
    start = pl.multiple_of(me * (2 * width), 2 * width)
    here = neighbours(spacing_z[:, pl.ds(start, 2 * width)])
    earlier = pl.multiple_of(jnp.maximum(start - width, 0), width)
    previous = spacing_z[:, pl.ds(earlier, width)]
    lane = lax.broadcasted_iota(jnp.int32, (1, width), 1)
    inside = jnp.where(me > 0, 1.0, 0.0)
    first = lane == 0
    even_before = jnp.where(first, inside * previous[:, width - 2 : width - 1], here[2])
    odd_before = jnp.where(first, inside * previous[:, width - 1 : width], here[3])
    coefz[...] = jnp.zeros_like(coefz)
    for k, row in enumerate(coefficients(here[0], here[1], even_before, odd_before)):
        coefz[k : k + 1, :] = row

    blocks = targets.shape[1]
    member = lax.broadcasted_iota(jnp.int32, (group, blocks), 0)
    named = jnp.where(member == targets[...], 1.0, 0.0)
    before = lax.broadcasted_iota(jnp.int32, (blocks, blocks), 0)
    after = lax.broadcasted_iota(jnp.int32, (blocks, blocks), 1)
    counted = jnp.dot(
        named.astype(jnp.bfloat16),
        jnp.where(before < after, 1.0, 0.0).astype(jnp.bfloat16),
        preferred_element_type=jnp.float32,
    )
    slot = jnp.sum(named * counted, axis=0, keepdims=True).astype(jnp.int32)
    place = targets[...] * capacity + slot
    header[...] = jnp.zeros_like(header)
    if listed:
        direct = capacity // 2
        there = 1 - lax.axis_index("gy") // 2
        tally = jnp.sum(named, axis=1, keepdims=True)
        kind = lax.broadcasted_iota(jnp.int32, (group, 1), 0)
        more = jnp.where(kind // 4 == there, jnp.maximum(tally - direct, 0.0), 0.0)
        ahead = jnp.sum(jnp.where(member < targets[...], more, 0.0), axis=0, keepdims=True)
        listing = group * capacity + 1 - direct + ahead.astype(jnp.int32) + slot
        place = jnp.where((targets[...] // 4 == there) & (slot >= direct), listing, place)
        side = lax.broadcasted_iota(jnp.int32, (group, 128), 0)
        across = lax.broadcasted_iota(jnp.int32, (group, 128), 1)
        header[0:1, :] = jnp.sum(jnp.where(side == across, more, 0.0), axis=0, keepdims=True)
        scalars[9 + half : 10 + half, :] = jnp.sum(more, axis=0, keepdims=True) + jnp.zeros(
            (1, 128), jnp.float32
        )
    placed[...] = place


class Table:
    def __init__(self, scalars):
        self.scalars = scalars

    def __getitem__(self, place):
        return self.scalars[8 + place[0], place[1]]


def exchange_first(
    count, over, scalars, hbm_nodes, out, most, nodes, left, right, send, tails, needs, wants,
    send_sem, recv_sem, need_send, need_recv, want_send, want_recv, load_sem,
):
    me, row = lax.axis_index("gx"), lax.axis_index("gy")
    load = pltpu.make_async_copy(hbm_nodes, nodes, load_sem)
    load.start()
    half = nodes.shape[0] // 2
    lines = nodes.shape[1]
    barrier = pltpu.get_barrier_semaphore()
    for d in range(1, count):
        pl.semaphore_signal(
            barrier, inc=1, device_id={"gx": lax.rem(me + d, count)}, device_id_type=MESH
        )
    for d in range(1, over):
        pl.semaphore_signal(
            barrier, inc=1, device_id={"gy": lax.rem(row + d, over)}, device_id_type=MESH
        )

    def coef(kind, k):
        return scalars[kind, me * half + k]

    factor = Table(scalars)
    gain_last = scalars[8 + half, half - 1]
    needs[0] = jnp.full(needs.shape[1:], scalars[9 + half, 0], jnp.float32)
    load.wait()

    last = half - 1
    send[1, pl.ds(0, lines), :] = nodes[2 * last + 1] - coef(0, last) * nodes[2 * last]
    pl.semaphore_wait(barrier, count + over - 2)

    to_right = pltpu.make_async_remote_copy(
        src_ref=send.at[1, pl.ds(0, lines)], dst_ref=left, send_sem=send_sem.at[0], recv_sem=recv_sem.at[0],
        device_id={"gx": lax.rem(me + 1, count)}, device_id_type=MESH,
    )
    to_left = pltpu.make_async_remote_copy(
        src_ref=nodes.at[0], dst_ref=right, send_sem=send_sem.at[1], recv_sem=recv_sem.at[1],
        device_id={"gx": lax.rem(me + count - 1, count)}, device_id_type=MESH,
    )

    @pl.when(me < count - 1)
    def _():
        to_right.start()

    @pl.when(me > 0)
    def _():
        to_left.start()

    small = []
    for d in range(1, count):
        small.append(
            pltpu.make_async_remote_copy(
                src_ref=needs.at[0], dst_ref=needs.at[d],
                send_sem=need_send.at[d], recv_sem=need_recv.at[d],
                device_id={"gx": lax.rem(me + d, count)}, device_id_type=MESH,
            )
        )
        small[-1].start()

    weights = []
    for k in range(half):
        weight = factor[last, k] * coef(2, k)
        if k < last:
            weight = weight + factor[last, k + 1] * coef(3, k + 1)
        weights.append(weight)
    edge = factor[last, 0] * coef(3, 0)

    def chunk(i, carry):
        rows = pl.ds(pl.multiple_of(i * 8, 8), 8)
        even = nodes[0, rows, :]
        value = (-edge * coef(5, 0)) * even
        for k in range(half):
            detail = nodes[2 * k + 1, rows, :] - coef(0, k) * even
            if k < last:
                even = nodes[2 * k + 2, rows, :]
                detail = detail - coef(1, k) * even
            value = value + weights[k] * detail
        send[0, rows, :] = value
        return carry

    lax.fori_loop(0, lines // 8, chunk, 0)
    for one in small:
        one.wait_recv()
    wants[0] = jnp.max(needs[...], axis=0)
    for d in range(1, over):
        small.append(
            pltpu.make_async_remote_copy(
                src_ref=wants.at[0], dst_ref=wants.at[d],
                send_sem=want_send.at[d], recv_sem=want_recv.at[d],
                device_id={"gy": lax.rem(row + d, over)}, device_id_type=MESH,
            )
        )
        small[-1].start()

    @pl.when(me == 0)
    def _():
        left[...] = jnp.zeros_like(left)

    @pl.when(me == count - 1)
    def _():
        right[...] = jnp.zeros_like(right)

    @pl.when(me > 0)
    def _():
        to_right.wait_recv()

    @pl.when(me < count - 1)
    def _():
        to_left.wait_recv()

    end = -(factor[last, last] * coef(2, last)) * coef(1, last)
    own = send.at[0]
    own[pl.ds(0, lines), :] = own[pl.ds(0, lines), :] + edge * left[...] + end * right[...]
    own[pl.ds(lines, 8), :] = jnp.full((8, own.shape[1]), gain_last, jnp.float32)

    copies = []
    for d in range(1, count):
        copies.append(
            pltpu.make_async_remote_copy(
                src_ref=tails.at[0], dst_ref=tails.at[d],
                send_sem=send_sem.at[1 + d], recv_sem=recv_sem.at[1 + d],
                device_id={"gx": lax.rem(me + d, count)}, device_id_type=MESH,
            )
        )
    tails[0] = own[...]
    for d in range(1, count):

        @pl.when(me + d < count)
        def _(d=d):
            copies[d - 1].start()

    out[0] = left[...]
    out[1] = right[...]
    out[2] = jnp.zeros_like(left)
    for d in range(count - 1, 0, -1):

        @pl.when(me >= d)
        def _(d=d):
            copies[d - 1].wait_recv()
            out[2] = (
                tails[d, pl.ds(0, lines), :]
                + jnp.max(tails[d, pl.ds(lines, 8), :], axis=0, keepdims=True) * out[2]
            )

    for one in small[count - 1 :]:
        one.wait_recv()
    most[...] = jnp.max(wants[...], axis=0)
    for one in small:
        one.wait_send()

    @pl.when(me < count - 1)
    def _():
        to_right.wait_send()

    @pl.when(me > 0)
    def _():
        to_left.wait_send()

    for d in range(1, count):

        @pl.when(me + d < count)
        def _(d=d):
            copies[d - 1].wait_send()


def loads(coefz):
    width = coefz.shape[1]
    row = lax.broadcasted_iota(jnp.int32, (2 * width, width), 0)
    twice = 2 * lax.broadcasted_iota(jnp.int32, (2 * width, width), 1)
    a, b, half_even, half_odd, a_before, b_before = [coefz[k : k + 1, :] for k in range(6)]
    zero = jnp.zeros((2 * width, width), jnp.float32)
    detail = jnp.where(row == twice, -a, zero)
    detail = jnp.where(row == twice + 1, 1.0, detail)
    detail = jnp.where(row == twice + 2, -b, detail)
    earlier = jnp.where(row == twice - 2, -a_before, zero)
    earlier = jnp.where(row == twice - 1, 1.0, earlier)
    earlier = jnp.where(row == twice, -b_before, earlier)
    return detail, half_even * detail + half_odd * earlier, row == twice


def first_kernel(
    nodes, planes, most, scalars, coefz, factor_z, gain_z, detail, coarse, payload, weights,
    *, count,
):
    me = lax.axis_index("gx")
    half = detail.shape[0]
    factor = Table(scalars)

    def coef(row, k):
        return scalars[row, me * half + k]

    width = factor_z.shape[0]

    @pl.when(pl.program_id(0) == 0)
    def _():
        load = loads(coefz)[1]
        tail = lax.dot_general(
            factor_z[pl.ds(width - 8, 8), :], load, (((1,), (1,)), ((), ())), precision=HIGHEST
        )
        lane = lax.broadcasted_iota(jnp.int32, (1, 2 * width), 1)
        a_last = coefz[0:1, width - 1 : width]
        weights[...] = jnp.zeros_like(weights)
        weights[0:1, :] = jnp.where(lane == 0, 1.0, 0.0)
        weights[1:2, :] = jnp.where(
            lane == 2 * width - 2, -a_last, jnp.where(lane == 2 * width - 1, 1.0, 0.0)
        )
        weights[2:3, :] = tail[7:8, :]

    for i in range(nodes.shape[1] // 8):
        rows = pl.ds(i * 8, 8)
        even = [nodes[2 * k, rows, :] for k in range(half)]
        before = planes[0, rows, :] - coef(5, 0) * even[0]
        load = []
        for k in range(half):
            after = even[k + 1] if k + 1 < half else planes[1, rows, :]
            value = nodes[2 * k + 1, rows, :] - coef(0, k) * even[k] - coef(1, k) * after
            detail[k, rows, :] = value
            load.append(coef(2, k) * value + coef(3, k) * before)
            before = value
        for k in range(half):
            value = nodes[2 * k, rows, :] + scalars[8 + half, k] * planes[2, rows, :]
            for j in range(half):
                value = value + factor[k, j] * load[j]
            coarse[k, rows, :] = value

    lines = coarse[...].reshape(half * coarse.shape[1], coarse.shape[2])
    sent = lax.dot_general(
        weights[...], lines, (((1,), (1,)), ((), ())), precision=HIGHEST
    )
    kind = lax.broadcasted_iota(jnp.int32, sent.shape, 0)
    end_gain = gain_z[0:1, width - 1 : width]
    end_first = factor_z[width - 1 : width, 0:1] * coefz[3:4, 0:1]
    end_last = -(
        factor_z[width - 1 : width, width - 1 : width]
        * coefz[2:3, width - 1 : width]
        * coefz[1:2, width - 1 : width]
    )
    sent = jnp.where(kind == 3, end_gain, sent)
    sent = jnp.where(kind == 4, end_first, sent)
    sent = jnp.where(kind == 5, end_last, sent)
    sent = jnp.where(kind == 6, most[0:1, 0:1], sent)
    payload[0] = sent


def third_kernel(
    placed, coarse, gathered, coefz, factor_z, gain_z, header, detail, outgoing, level, matrix,
    update, tiles, *, count, chunks, levels, head,
):
    me = lax.axis_index("gz")
    step = pl.program_id(0)
    width = factor_z.shape[0]

    @pl.when(step == 0)
    def _():
        outgoing[...] = jnp.zeros_like(outgoing)
        outgoing[head] = header[...]
        need = jnp.max(gathered[:, 0, 6:7, :])
        level[0] = sum((need > sent).astype(jnp.int32) for sent in levels)
        detail_of, load_of, is_even = loads(coefz)
        solved = lax.dot_general(
            load_of, factor_z[...], (((1,), (1,)), ((), ())), precision=HIGHEST
        )
        matrix[:, 0:width] = jnp.where(is_even, 1.0, 0.0) + solved
        matrix[:, width:] = detail_of
        turned = factor_z[...].T
        b_last = coefz[1:2, width - 1 : width]
        lane = lax.broadcasted_iota(jnp.int32, (1, width), 1)
        update[...] = jnp.zeros_like(update)
        update[0:1, 0:width] = -turned[width - 1 : width, :] * (
            coefz[2:3, width - 1 : width] * b_last
        )
        update[0:1, width:] = jnp.where(lane == width - 1, -b_last, 0.0)
        update[1:2, 0:width] = turned[0:1, :] * coefz[3:4, 0:1]
        update[2:3, 0:width] = gain_z[...]

    def heard(p, row):
        return gathered[p, 0, row : row + 1, :]

    empty = jnp.zeros_like(heard(0, 0))
    right, left, carry = empty, empty, empty
    for p in range(count):
        right = jnp.where(me + 1 == p, heard(p, 0), right)
        left = jnp.where(me - 1 == p, heard(p, 1), left)
        if p < count - 1:
            tail = heard(p, 2) + heard(p, 5) * heard(p + 1, 0) + heard(p, 3) * carry
            if p > 0:
                tail = tail + heard(p, 4) * heard(p - 1, 1)
            carry = jnp.where(p < me, tail, carry)
    kind = lax.broadcasted_iota(jnp.int32, (8, empty.shape[1]), 0)
    edges = jnp.where(kind == 0, right, jnp.where(kind == 1, left, jnp.where(kind == 2, carry, 0.0)))

    rows = coarse.shape[0] * coarse.shape[1]
    lines = coarse[...].reshape(rows, coarse.shape[2])
    result = jnp.dot(lines, matrix[...], precision=HIGHEST) + lax.dot_general(
        edges, update[...], (((0,), (0,)), ((), ())), precision=HIGHEST
    )
    upper = result[:, :width].reshape(rows // 8, 8, width)
    lower = result[:, width:].reshape(rows // 8, 8, width)
    detail[...] = result[:, width:].reshape(detail.shape)
    top = lax.broadcasted_iota(jnp.int32, upper.shape, 1) < LINES
    tiles[0] = jnp.where(top, upper, pltpu.roll(lower, LINES, 1))
    tiles[1] = jnp.where(top, pltpu.roll(upper, LINES, 1), lower)
    eights = coarse.shape[1] // 8

    def scatter(x, carry):
        for j in range(eights):
            for half in range(2):
                block = x * (2 * eights * chunks) + step * (2 * eights) + 2 * j + half
                outgoing[placed[0, block]] = tiles[half, x * eights + j]
        return carry

    lax.fori_loop(0, coarse.shape[0], scatter, 0)


def deliver_kernel(n_gy, n_gz, outgoing, received, send_sem, recv_sem, own_sem):
    gy, gz = lax.axis_index("gy"), lax.axis_index("gz")
    me = gy * n_gz + gz
    shifts = [
        (dy, dz) for dy in range(n_gy) for dz in range(n_gz) if dy + dz > 0
    ]
    shifts.sort(key=lambda shift: -min(shift[0], n_gy - shift[0]))
    barrier = pltpu.get_barrier_semaphore()
    targets = []
    for dy, dz in shifts:
        there = (lax.rem(gy + dy, n_gy), lax.rem(gz + dz, n_gz))
        targets.append(there)
        pl.semaphore_signal(
            barrier, inc=1, device_id={"gy": there[0], "gz": there[1]}, device_id_type=MESH
        )
    own = pltpu.make_async_copy(outgoing.at[me], received.at[me], own_sem)
    own.start()
    pl.semaphore_wait(barrier, len(shifts))
    copies = []
    for k, there in enumerate(targets):
        copy = pltpu.make_async_remote_copy(
            src_ref=outgoing.at[there[0] * n_gz + there[1]],
            dst_ref=received.at[me],
            send_sem=send_sem.at[k],
            recv_sem=recv_sem.at[k],
            device_id={"gy": there[0], "gz": there[1]},
            device_id_type=MESH,
        )
        copy.start()
        copies.append(copy)
    own.wait()
    for copy in copies:
        copy.wait()


def spread_kernel(sent, outgoing, received, lists, send_sem, recv_sem, own_sem):
    gy, gz = lax.axis_index("gy"), lax.axis_index("gz")
    half, place = gy // 2, lax.rem(gy, 2)
    me = gy * 2 + gz
    capacity = received.shape[1]

    def at(step):
        h, y, z = step
        there_half = 1 - half if h else half
        there_place = 1 - place if y else place
        return there_half * 2 + there_place, 1 - gz if z else gz

    steps = [(h, y, z) for h in (0, 1) for y in (0, 1) for z in (0, 1) if h + y + z]
    barrier = pltpu.get_barrier_semaphore()
    for step in steps:
        there = at(step)
        pl.semaphore_signal(
            barrier, inc=1, device_id={"gy": there[0], "gz": there[1]}, device_id_type=MESH
        )
    own = pltpu.make_async_copy(
        outgoing.at[pl.ds(me * capacity, capacity)], received.at[me], own_sem
    )
    own.start()
    pl.semaphore_wait(barrier, len(steps))

    def copy(k, step, source, target):
        there = at(step)
        return pltpu.make_async_remote_copy(
            src_ref=source, dst_ref=target, send_sem=send_sem.at[k], recv_sem=recv_sem.at[k],
            device_id={"gy": there[0], "gz": there[1]}, device_id_type=MESH,
        )

    def direct(step):
        there = at(step)
        count = capacity // 2 if step[0] else capacity
        return copy(
            steps.index(step), step,
            outgoing.at[pl.ds((there[0] * 2 + there[1]) * capacity, count)],
            received.at[me, pl.ds(0, count)],
        )

    mine, beside = place * 2 + gz, (1 - place) * 2 + gz
    rows = pl.ds(0, 1 + sent)
    tail = pl.ds(received.shape[0] * capacity, 1 + sent)
    across = copy(7, (1, 0, 0), outgoing.at[tail], lists.at[mine, rows])
    along = copy(8, (0, 1, 0), lists.at[mine, rows], lists.at[mine, rows])
    to_core = copy(9, (0, 0, 1), lists.at[mine, rows], lists.at[mine, rows])
    to_core_too = copy(10, (0, 0, 1), lists.at[beside, rows], lists.at[beside, rows])
    early = [direct((0, 1, 0)), direct((0, 0, 1))]
    late = [direct(step) for step in ((1, 0, 0), (1, 0, 1), (1, 1, 0), (1, 1, 1), (0, 1, 1))]
    across.start()
    for one in early:
        one.start()
    across.wait_recv()
    along.start()
    to_core.start()
    for one in late:
        one.start()
    along.wait_recv()
    to_core_too.start()
    own.wait()
    across.wait_send()
    along.wait_send()
    for one in early + late + [to_core, to_core_too]:
        one.wait()


def gather_kernel(sent, base, hbm_lists, received, lists, tiles, sems):
    direct = tiles.shape[1] // 2
    half = lax.axis_index("gy") // 2
    me = lax.axis_index("gy") * 2 + lax.axis_index("gz")
    rows = pl.ds(0, 1 + sent)
    near = [half * 4 + k for k in range(4)]
    far = [(1 - half) * 4 + k for k in range(4)]
    low = pl.ds(0, direct)
    whole = [
        pltpu.make_async_copy(base.at[near[k]], tiles.at[k], sems.at[0, k]) for k in range(4)
    ]
    listed = [
        pltpu.make_async_copy(hbm_lists.at[k, rows], lists.at[k, rows], sems.at[1, k])
        for k in range(4)
    ]
    part = [
        pltpu.make_async_copy(base.at[far[k], low], tiles.at[4 + k, low], sems.at[2, k])
        for k in range(4)
    ]
    stores = [
        pltpu.make_async_copy(tiles.at[k], received.at[(near + far)[k]], sems.at[3 + k // 4, k % 4])
        for k in range(8)
    ]
    for one in whole + listed + part:
        one.start()
    for k in range(4):
        whole[k].wait()
        stores[k].start()
    for k in range(4):
        listed[k].wait()
        part[k].wait()
        header = lists[k, 0, 0:1, :]
        lane = lax.broadcasted_iota(jnp.int32, header.shape, 1)
        start = jnp.sum(jnp.where((lane >= half * 4) & (lane < me), header, 0.0))
        count = jnp.sum(jnp.where(lane == me, header, 0.0)).astype(jnp.int32)
        later = lists[k, pl.ds(1 + start.astype(jnp.int32), direct)]
        slot = lax.broadcasted_iota(jnp.int32, later.shape, 0)
        tiles[4 + k, pl.ds(direct, direct)] = jnp.where(slot < count, later, 0.0)
        stores[4 + k].start()
    for one in stores:
        one.wait()


def spread(outgoing, group, room, levels, level):
    capacity = (outgoing.shape[0] - room - 1) // group
    tile = outgoing.shape[1:]
    def branch(number, sent):
        def run(outgoing):
            base, lists = pl.pallas_call(
                functools.partial(spread_kernel, sent),
                out_shape=[
                    jax.ShapeDtypeStruct((group, capacity) + tile, jnp.float32),
                    jax.ShapeDtypeStruct((group // 2, room + 1) + tile, jnp.float32),
                ],
                in_specs=[pl.BlockSpec(memory_space=pl.ANY)],
                out_specs=[pl.BlockSpec(memory_space=pl.ANY)] * 2,
                scratch_shapes=[
                    pltpu.SemaphoreType.DMA((11,)),
                    pltpu.SemaphoreType.DMA((11,)),
                    pltpu.SemaphoreType.DMA,
                ],
                compiler_params=pltpu.CompilerParams(
                    collective_id=2 + number, has_side_effects=True
                ),
                name="spread",
            )(outgoing)
            return pl.pallas_call(
                functools.partial(gather_kernel, sent),
                in_specs=[pl.BlockSpec(memory_space=pl.ANY)] * 2,
                out_specs=pl.BlockSpec(memory_space=pltpu.HBM),
                scratch_shapes=[
                    pltpu.VMEM((group // 2, room + 1) + tile, jnp.float32),
                    pltpu.VMEM((group, capacity) + tile, jnp.float32),
                    pltpu.SemaphoreType.DMA((5, group // 2)),
                ],
                out_shape=jax.ShapeDtypeStruct(base.shape, jnp.float32),
                compiler_params=pltpu.CompilerParams(vmem_limit_bytes=LIMIT),
                name="gather",
            )(base, lists)

        return run

    branches = [branch(k, sent) for k, sent in enumerate(levels + (room,))]
    return lax.switch(level, branches, outgoing)


def local(sizes, nodes, spacing_x, spacing_z, factor_x, gain_x, factor_z, gain_z, receivers):
    n_gx, n_gy, n_gz = sizes
    length, lines, depth = nodes.shape
    half, width = length // 2, depth // 2
    group = n_gy * n_gz
    blocks = half * lines // LINES
    capacity = max(2, blocks // group * 2)
    listed = n_gy == 4 and n_gz == 2
    direct = capacity // 2
    room = group // 2 * (capacity - direct) if listed else 0
    levels = tuple(room * k // 32 for k in (12, 16, 19))
    scalars, coefz, placed, header = pl.pallas_call(
        functools.partial(prepare_kernel, group=group, capacity=capacity, listed=listed),
        out_shape=[
            jax.ShapeDtypeStruct((32, 128), jnp.float32),
            jax.ShapeDtypeStruct((8, width), jnp.float32),
            jax.ShapeDtypeStruct((1, blocks), jnp.int32),
            jax.ShapeDtypeStruct((2 * LINES, 128), jnp.float32),
        ],
        compiler_params=pltpu.CompilerParams(vmem_limit_bytes=LIMIT),
        name="prepare",
    )(
        spacing_x.reshape(1, -1), spacing_z.reshape(1, -1), factor_x, gain_x.reshape(1, -1),
        receivers.reshape(1, -1),
    )
    gain_row = gain_z.reshape(1, width)
    vmem = pl.BlockSpec(memory_space=pltpu.VMEM)
    smem = pl.BlockSpec(memory_space=pltpu.SMEM)
    hbm = pl.BlockSpec(memory_space=pl.ANY)

    planes, most = pl.pallas_call(
        functools.partial(exchange_first, n_gx, n_gy),
        out_shape=[
            jax.ShapeDtypeStruct((3, lines, depth), jnp.float32),
            jax.ShapeDtypeStruct((8, 128), jnp.float32),
        ],
        in_specs=[smem, hbm],
        out_specs=[vmem, vmem],
        scratch_shapes=[
            pltpu.VMEM((length, lines, depth), jnp.float32),
            pltpu.VMEM((lines, depth), jnp.float32),
            pltpu.VMEM((lines, depth), jnp.float32),
            pltpu.VMEM((2, lines + 8, depth), jnp.float32),
            pltpu.VMEM((n_gx, lines + 8, depth), jnp.float32),
            pltpu.VMEM((n_gx, 8, 128), jnp.float32),
            pltpu.VMEM((n_gy, 8, 128), jnp.float32),
            pltpu.SemaphoreType.DMA((n_gx + 1,)),
            pltpu.SemaphoreType.DMA((n_gx + 1,)),
            pltpu.SemaphoreType.DMA((n_gx,)),
            pltpu.SemaphoreType.DMA((n_gx,)),
            pltpu.SemaphoreType.DMA((n_gy,)),
            pltpu.SemaphoreType.DMA((n_gy,)),
            pltpu.SemaphoreType.DMA,
        ],
        compiler_params=pltpu.CompilerParams(
            collective_id=0, has_side_effects=True, vmem_limit_bytes=LIMIT
        ),
        name="exchange_first",
    )(scalars, nodes)

    chunks = 4
    rows = lines // chunks
    params = pltpu.CompilerParams(
        dimension_semantics=("arbitrary",), vmem_limit_bytes=LIMIT
    )
    detail_x, coarse_x, payload = pl.pallas_call(
        functools.partial(first_kernel, count=n_gx),
        grid=(chunks,),
        in_specs=[
            pl.BlockSpec((length, rows, depth), lambda i: (0, i, 0)),
            pl.BlockSpec((3, rows, depth), lambda i: (0, i, 0)),
            pl.BlockSpec((8, 128), lambda i: (0, 0)),
            smem,
            pl.BlockSpec((8, width), lambda i: (0, 0)),
            pl.BlockSpec((width, width), lambda i: (0, 0)),
            pl.BlockSpec((1, width), lambda i: (0, 0)),
        ],
        out_specs=[
            pl.BlockSpec((half, rows, depth), lambda i: (0, i, 0)),
            pl.BlockSpec((half, rows, depth), lambda i: (0, i, 0)),
            pl.BlockSpec((1, 8, half * rows), lambda i: (i, 0, 0)),
        ],
        out_shape=[
            jax.ShapeDtypeStruct((half, lines, depth), jnp.float32),
            jax.ShapeDtypeStruct((half, lines, depth), jnp.float32),
            jax.ShapeDtypeStruct((chunks, 8, half * rows), jnp.float32),
        ],
        scratch_shapes=[pltpu.VMEM((8, depth), jnp.float32)],
        compiler_params=params,
        name="pass_first",
    )(nodes, planes, most, scalars, coefz, factor_z, gain_row)

    gathered = lax.all_gather(payload, "gz")

    held = group * capacity + (room + 1 if listed else 1)
    detail_z, outgoing, level = pl.pallas_call(
        functools.partial(
            third_kernel, count=n_gz, chunks=chunks, levels=levels, head=group * capacity
        ),
        grid=(chunks,),
        in_specs=[
            smem,
            pl.BlockSpec((half, rows, depth), lambda i: (0, i, 0)),
            pl.BlockSpec((n_gz, 1, 8, half * rows), lambda i: (0, i, 0, 0)),
            pl.BlockSpec((8, width), lambda i: (0, 0)),
            pl.BlockSpec((width, width), lambda i: (0, 0)),
            pl.BlockSpec((1, width), lambda i: (0, 0)),
            pl.BlockSpec((2 * LINES, width), lambda i: (0, 0)),
        ],
        out_specs=[
            pl.BlockSpec((half, rows, width), lambda i: (0, i, 0)),
            pl.BlockSpec((held, 2 * LINES, width), lambda i: (0, 0, 0)),
            smem,
        ],
        out_shape=[
            jax.ShapeDtypeStruct((half, lines, width), jnp.float32),
            jax.ShapeDtypeStruct((held, 2 * LINES, width), jnp.float32),
            jax.ShapeDtypeStruct((1,), jnp.int32),
        ],
        scratch_shapes=[
            pltpu.VMEM((depth, depth), jnp.float32),
            pltpu.VMEM((8, depth), jnp.float32),
            pltpu.VMEM((2, half * rows // 8, 8, width), jnp.float32),
        ],
        compiler_params=params,
        name="pass_third",
    )(placed, coarse_x, gathered, coefz, factor_z, gain_row, header)

    if listed:
        received = spread(outgoing, group, room, levels, level[0])
    else:
        outgoing = outgoing[: group * capacity].reshape(group, capacity, 2 * LINES, width)
        received = pl.pallas_call(
            functools.partial(deliver_kernel, n_gy, n_gz),
            out_shape=jax.ShapeDtypeStruct(outgoing.shape, jnp.float32),
            in_specs=[hbm],
            out_specs=hbm,
            scratch_shapes=[
                pltpu.SemaphoreType.DMA((group - 1,)),
                pltpu.SemaphoreType.DMA((group - 1,)),
                pltpu.SemaphoreType.DMA,
            ],
            compiler_params=pltpu.CompilerParams(collective_id=1, has_side_effects=True),
            name="deliver",
        )(outgoing)
    return (
        detail_x,
        detail_z,
        received.reshape(1, group, capacity, 2, LINES, width),
    )


def solution(mesh):
    sizes = tuple(mesh.shape[axis] for axis in ("gx", "gy", "gz"))
    return jax.shard_map(
        functools.partial(local, sizes),
        mesh=mesh,
        in_specs=(
            P("gx", "gy", "gz"),
            P(),
            P(),
            P("gx", None),
            P("gx"),
            P("gz", None),
            P("gz"),
            P(("gx", "gy", "gz"), None),
        ),
        out_specs=(
            P("gx", "gy", "gz"),
            P("gx", "gy", "gz"),
            P(("gx", "gy", "gz"), None, None, None, None, None),
        ),
        check_vma=False,
    )
```

```python
import functools

import jax
import jax.numpy as jnp
from jax import lax
from jax.experimental import pallas as pl
from jax.experimental.pallas import tpu as pltpu
from jax.sharding import PartitionSpec as P

LINES = 4
MESH = pl.DeviceIdType.MESH
HIGHEST = lax.Precision.HIGHEST
LIMIT = 56 * 1024 * 1024


def neighbours(spacing):
    count = spacing.shape[1]
    parts, rest = [], spacing
    for _ in range(3):
        part = rest.astype(jnp.bfloat16).astype(jnp.float32)
        parts.append(part)
        rest = rest - part
    kind = lax.broadcasted_iota(jnp.int32, (16, count), 0)
    stacked = jnp.zeros((16, count), jnp.float32)
    for k, part in enumerate(parts):
        stacked = jnp.where(kind == k, part, stacked)
    row = lax.broadcasted_iota(jnp.int32, (count, 128), 0)
    twice = 2 * lax.broadcasted_iota(jnp.int32, (count, 128), 1)
    chosen = [
        jnp.dot(
            stacked.astype(jnp.bfloat16),
            jnp.where(row == twice + shift, 1.0, 0.0).astype(jnp.bfloat16),
            preferred_element_type=jnp.float32,
        )
        for shift in (0, 1, -2, -1)
    ]
    return [jnp.sum(one, axis=0, keepdims=True) for one in chosen]


def coefficients(even, odd, even_before, odd_before):
    def parts(even, odd):
        total = even + odd
        total = jnp.where(total > 0, total, 1.0)
        return odd / total, even / total

    return (
        parts(even, odd) + (0.5 * even, 0.5 * odd_before) + parts(even_before, odd_before)
    )


def prepare_kernel(
    spacing_x, spacing_z, factor, gain, targets, scalars, coefz, placed, header, *, group,
    capacity, listed,
):
    half = factor.shape[0]
    scalars[...] = jnp.zeros_like(scalars)
    for k, row in enumerate(coefficients(*neighbours(spacing_x[...]))):
        scalars[k : k + 1, :] = row
    scalars[8 : 8 + half, 0:half] = factor[...]
    scalars[8 + half : 9 + half, 0:half] = gain[...]

    me = lax.axis_index("gz")
    width = coefz.shape[1]
    start = pl.multiple_of(me * (2 * width), 2 * width)
    here = neighbours(spacing_z[:, pl.ds(start, 2 * width)])
    earlier = pl.multiple_of(jnp.maximum(start - width, 0), width)
    previous = spacing_z[:, pl.ds(earlier, width)]
    lane = lax.broadcasted_iota(jnp.int32, (1, width), 1)
    inside = jnp.where(me > 0, 1.0, 0.0)
    first = lane == 0
    even_before = jnp.where(first, inside * previous[:, width - 2 : width - 1], here[2])
    odd_before = jnp.where(first, inside * previous[:, width - 1 : width], here[3])
    coefz[...] = jnp.zeros_like(coefz)
    for k, row in enumerate(coefficients(here[0], here[1], even_before, odd_before)):
        coefz[k : k + 1, :] = row

    blocks = targets.shape[1]
    member = lax.broadcasted_iota(jnp.int32, (group, blocks), 0)
    named = jnp.where(member == targets[...], 1.0, 0.0)
    before = lax.broadcasted_iota(jnp.int32, (blocks, blocks), 0)
    after = lax.broadcasted_iota(jnp.int32, (blocks, blocks), 1)
    counted = jnp.dot(
        named.astype(jnp.bfloat16),
        jnp.where(before < after, 1.0, 0.0).astype(jnp.bfloat16),
        preferred_element_type=jnp.float32,
    )
    slot = jnp.sum(named * counted, axis=0, keepdims=True).astype(jnp.int32)
    place = targets[...] * capacity + slot
    header[...] = jnp.zeros_like(header)
    if listed:
        direct = capacity // 2
        there = 1 - lax.axis_index("gy") // 2
        tally = jnp.sum(named, axis=1, keepdims=True)
        kind = lax.broadcasted_iota(jnp.int32, (group, 1), 0)
        more = jnp.where(kind // 4 == there, jnp.maximum(tally - direct, 0.0), 0.0)
        ahead = jnp.sum(jnp.where(member < targets[...], more, 0.0), axis=0, keepdims=True)
        listing = group * capacity + 1 - direct + ahead.astype(jnp.int32) + slot
        place = jnp.where((targets[...] // 4 == there) & (slot >= direct), listing, place)
        side = lax.broadcasted_iota(jnp.int32, (group, 128), 0)
        across = lax.broadcasted_iota(jnp.int32, (group, 128), 1)
        header[0:1, :] = jnp.sum(jnp.where(side == across, more, 0.0), axis=0, keepdims=True)
        scalars[9 + half : 10 + half, :] = jnp.sum(more, axis=0, keepdims=True) + jnp.zeros(
            (1, 128), jnp.float32
        )
    placed[...] = place


class Table:
    def __init__(self, scalars):
        self.scalars = scalars

    def __getitem__(self, place):
        return self.scalars[8 + place[0], place[1]]


def exchange_first(
    count, over, scalars, hbm_nodes, out, most, nodes, left, right, send, tails, needs, wants,
    send_sem, recv_sem, need_send, need_recv, want_send, want_recv, load_sem,
):
    me, row = lax.axis_index("gx"), lax.axis_index("gy")
    ends = pl.ds(nodes.shape[0] - 2, 2)
    body = pl.ds(0, nodes.shape[0] - 2)
    load_ends = pltpu.make_async_copy(hbm_nodes.at[ends], nodes.at[ends], load_sem.at[0])
    load_body = pltpu.make_async_copy(hbm_nodes.at[body], nodes.at[body], load_sem.at[1])
    load_ends.start()
    load_body.start()
    half = nodes.shape[0] // 2
    lines = nodes.shape[1]
    barrier = pltpu.get_barrier_semaphore()
    for d in range(1, count):
        pl.semaphore_signal(
            barrier, inc=1, device_id={"gx": lax.rem(me + d, count)}, device_id_type=MESH
        )
    for d in range(1, over):
        pl.semaphore_signal(
            barrier, inc=1, device_id={"gy": lax.rem(row + d, over)}, device_id_type=MESH
        )

    def coef(kind, k):
        return scalars[kind, me * half + k]

    factor = Table(scalars)
    gain_last = scalars[8 + half, half - 1]
    needs[0] = jnp.full(needs.shape[1:], scalars[9 + half, 0], jnp.float32)
    load_ends.wait()

    last = half - 1
    send[1, pl.ds(0, lines), :] = nodes[2 * last + 1] - coef(0, last) * nodes[2 * last]
    pl.semaphore_wait(barrier, count + over - 2)

    to_right = pltpu.make_async_remote_copy(
        src_ref=send.at[1, pl.ds(0, lines)], dst_ref=left, send_sem=send_sem.at[0], recv_sem=recv_sem.at[0],
        device_id={"gx": lax.rem(me + 1, count)}, device_id_type=MESH,
    )
    to_left = pltpu.make_async_remote_copy(
        src_ref=hbm_nodes.at[0], dst_ref=right, send_sem=send_sem.at[1], recv_sem=recv_sem.at[1],
        device_id={"gx": lax.rem(me + count - 1, count)}, device_id_type=MESH,
    )

    @pl.when(me < count - 1)
    def _():
        to_right.start()

    @pl.when(me > 0)
    def _():
        to_left.start()

    small = []
    for d in range(1, count):
        small.append(
            pltpu.make_async_remote_copy(
                src_ref=needs.at[0], dst_ref=needs.at[d],
                send_sem=need_send.at[d], recv_sem=need_recv.at[d],
                device_id={"gx": lax.rem(me + d, count)}, device_id_type=MESH,
            )
        )
        small[-1].start()

    weights = []
    for k in range(half):
        weight = factor[last, k] * coef(2, k)
        if k < last:
            weight = weight + factor[last, k + 1] * coef(3, k + 1)
        weights.append(weight)
    edge = factor[last, 0] * coef(3, 0)

    def chunk(i, carry):
        rows = pl.ds(pl.multiple_of(i * 8, 8), 8)
        even = nodes[0, rows, :]
        value = (-edge * coef(5, 0)) * even
        for k in range(half):
            detail = nodes[2 * k + 1, rows, :] - coef(0, k) * even
            if k < last:
                even = nodes[2 * k + 2, rows, :]
                detail = detail - coef(1, k) * even
            value = value + weights[k] * detail
        send[0, rows, :] = value
        return carry

    load_body.wait()
    lax.fori_loop(0, lines // 8, chunk, 0)
    for one in small:
        one.wait_recv()
    wants[0] = jnp.max(needs[...], axis=0)
    for d in range(1, over):
        small.append(
            pltpu.make_async_remote_copy(
                src_ref=wants.at[0], dst_ref=wants.at[d],
                send_sem=want_send.at[d], recv_sem=want_recv.at[d],
                device_id={"gy": lax.rem(row + d, over)}, device_id_type=MESH,
            )
        )
        small[-1].start()

    @pl.when(me == 0)
    def _():
        left[...] = jnp.zeros_like(left)

    @pl.when(me == count - 1)
    def _():
        right[...] = jnp.zeros_like(right)

    @pl.when(me > 0)
    def _():
        to_right.wait_recv()

    @pl.when(me < count - 1)
    def _():
        to_left.wait_recv()

    end = -(factor[last, last] * coef(2, last)) * coef(1, last)
    own = send.at[0]
    own[pl.ds(0, lines), :] = own[pl.ds(0, lines), :] + edge * left[...] + end * right[...]
    own[pl.ds(lines, 8), :] = jnp.full((8, own.shape[1]), gain_last, jnp.float32)

    copies = []
    for d in range(1, count):
        copies.append(
            pltpu.make_async_remote_copy(
                src_ref=tails.at[0], dst_ref=tails.at[d],
                send_sem=send_sem.at[1 + d], recv_sem=recv_sem.at[1 + d],
                device_id={"gx": lax.rem(me + d, count)}, device_id_type=MESH,
            )
        )
    tails[0] = own[...]
    for d in range(1, count):

        @pl.when(me + d < count)
        def _(d=d):
            copies[d - 1].start()

    out[0] = left[...]
    out[1] = right[...]
    out[2] = jnp.zeros_like(left)
    for d in range(count - 1, 0, -1):

        @pl.when(me >= d)
        def _(d=d):
            copies[d - 1].wait_recv()
            out[2] = (
                tails[d, pl.ds(0, lines), :]
                + jnp.max(tails[d, pl.ds(lines, 8), :], axis=0, keepdims=True) * out[2]
            )

    for one in small[count - 1 :]:
        one.wait_recv()
    most[...] = jnp.max(wants[...], axis=0)
    for one in small:
        one.wait_send()

    @pl.when(me < count - 1)
    def _():
        to_right.wait_send()

    @pl.when(me > 0)
    def _():
        to_left.wait_send()

    for d in range(1, count):

        @pl.when(me + d < count)
        def _(d=d):
            copies[d - 1].wait_send()


def loads(coefz):
    width = coefz.shape[1]
    row = lax.broadcasted_iota(jnp.int32, (2 * width, width), 0)
    twice = 2 * lax.broadcasted_iota(jnp.int32, (2 * width, width), 1)
    a, b, half_even, half_odd, a_before, b_before = [coefz[k : k + 1, :] for k in range(6)]
    zero = jnp.zeros((2 * width, width), jnp.float32)
    detail = jnp.where(row == twice, -a, zero)
    detail = jnp.where(row == twice + 1, 1.0, detail)
    detail = jnp.where(row == twice + 2, -b, detail)
    earlier = jnp.where(row == twice - 2, -a_before, zero)
    earlier = jnp.where(row == twice - 1, 1.0, earlier)
    earlier = jnp.where(row == twice, -b_before, earlier)
    return detail, half_even * detail + half_odd * earlier, row == twice


def first_kernel(
    nodes, planes, most, scalars, coefz, factor_z, gain_z, detail, coarse, payload, weights,
    *, count,
):
    me = lax.axis_index("gx")
    half = detail.shape[0]
    factor = Table(scalars)

    def coef(row, k):
        return scalars[row, me * half + k]

    width = factor_z.shape[0]

    @pl.when(pl.program_id(0) == 0)
    def _():
        load = loads(coefz)[1]
        tail = lax.dot_general(
            factor_z[pl.ds(width - 8, 8), :], load, (((1,), (1,)), ((), ())), precision=HIGHEST
        )
        lane = lax.broadcasted_iota(jnp.int32, (1, 2 * width), 1)
        a_last = coefz[0:1, width - 1 : width]
        weights[...] = jnp.zeros_like(weights)
        weights[0:1, :] = jnp.where(lane == 0, 1.0, 0.0)
        weights[1:2, :] = jnp.where(
            lane == 2 * width - 2, -a_last, jnp.where(lane == 2 * width - 1, 1.0, 0.0)
        )
        weights[2:3, :] = tail[7:8, :]

    for i in range(nodes.shape[1] // 8):
        rows = pl.ds(i * 8, 8)
        even = [nodes[2 * k, rows, :] for k in range(half)]
        before = planes[0, rows, :] - coef(5, 0) * even[0]
        load = []
        for k in range(half):
            after = even[k + 1] if k + 1 < half else planes[1, rows, :]
            value = nodes[2 * k + 1, rows, :] - coef(0, k) * even[k] - coef(1, k) * after
            detail[k, rows, :] = value
            load.append(coef(2, k) * value + coef(3, k) * before)
            before = value
        for k in range(half):
            value = nodes[2 * k, rows, :] + scalars[8 + half, k] * planes[2, rows, :]
            for j in range(half):
                value = value + factor[k, j] * load[j]
            coarse[k, rows, :] = value

    lines = coarse[...].reshape(half * coarse.shape[1], coarse.shape[2])
    sent = lax.dot_general(
        weights[...], lines, (((1,), (1,)), ((), ())), precision=HIGHEST
    )
    kind = lax.broadcasted_iota(jnp.int32, sent.shape, 0)
    end_gain = gain_z[0:1, width - 1 : width]
    end_first = factor_z[width - 1 : width, 0:1] * coefz[3:4, 0:1]
    end_last = -(
        factor_z[width - 1 : width, width - 1 : width]
        * coefz[2:3, width - 1 : width]
        * coefz[1:2, width - 1 : width]
    )
    sent = jnp.where(kind == 3, end_gain, sent)
    sent = jnp.where(kind == 4, end_first, sent)
    sent = jnp.where(kind == 5, end_last, sent)
    sent = jnp.where(kind == 6, most[0:1, 0:1], sent)
    payload[0] = sent


def third_kernel(
    placed, coarse, gathered, coefz, factor_z, gain_z, header, detail, outgoing, level, matrix,
    update, tiles, *, count, chunks, levels, head,
):
    me = lax.axis_index("gz")
    step = pl.program_id(0)
    width = factor_z.shape[0]

    @pl.when(step == 0)
    def _():
        outgoing[...] = jnp.zeros_like(outgoing)
        outgoing[head] = header[...]
        need = jnp.max(gathered[:, 0, 6:7, :])
        level[0] = sum((need > sent).astype(jnp.int32) for sent in levels)
        detail_of, load_of, is_even = loads(coefz)
        solved = lax.dot_general(
            load_of, factor_z[...], (((1,), (1,)), ((), ())), precision=HIGHEST
        )
        matrix[:, 0:width] = jnp.where(is_even, 1.0, 0.0) + solved
        matrix[:, width:] = detail_of
        turned = factor_z[...].T
        b_last = coefz[1:2, width - 1 : width]
        lane = lax.broadcasted_iota(jnp.int32, (1, width), 1)
        update[...] = jnp.zeros_like(update)
        update[0:1, 0:width] = -turned[width - 1 : width, :] * (
            coefz[2:3, width - 1 : width] * b_last
        )
        update[0:1, width:] = jnp.where(lane == width - 1, -b_last, 0.0)
        update[1:2, 0:width] = turned[0:1, :] * coefz[3:4, 0:1]
        update[2:3, 0:width] = gain_z[...]

    def heard(p, row):
        return gathered[p, 0, row : row + 1, :]

    empty = jnp.zeros_like(heard(0, 0))
    right, left, carry = empty, empty, empty
    for p in range(count):
        right = jnp.where(me + 1 == p, heard(p, 0), right)
        left = jnp.where(me - 1 == p, heard(p, 1), left)
        if p < count - 1:
            tail = heard(p, 2) + heard(p, 5) * heard(p + 1, 0) + heard(p, 3) * carry
            if p > 0:
                tail = tail + heard(p, 4) * heard(p - 1, 1)
            carry = jnp.where(p < me, tail, carry)
    kind = lax.broadcasted_iota(jnp.int32, (8, empty.shape[1]), 0)
    edges = jnp.where(kind == 0, right, jnp.where(kind == 1, left, jnp.where(kind == 2, carry, 0.0)))

    rows = coarse.shape[0] * coarse.shape[1]
    lines = coarse[...].reshape(rows, coarse.shape[2])
    result = jnp.dot(lines, matrix[...], precision=HIGHEST) + lax.dot_general(
        edges, update[...], (((0,), (0,)), ((), ())), precision=HIGHEST
    )
    upper = result[:, :width].reshape(rows // 8, 8, width)
    lower = result[:, width:].reshape(rows // 8, 8, width)
    detail[...] = result[:, width:].reshape(detail.shape)
    top = lax.broadcasted_iota(jnp.int32, upper.shape, 1) < LINES
    tiles[0] = jnp.where(top, upper, pltpu.roll(lower, LINES, 1))
    tiles[1] = jnp.where(top, pltpu.roll(upper, LINES, 1), lower)
    eights = coarse.shape[1] // 8

    def scatter(x, carry):
        for j in range(eights):
            for half in range(2):
                block = x * (2 * eights * chunks) + step * (2 * eights) + 2 * j + half
                outgoing[placed[0, block]] = tiles[half, x * eights + j]
        return carry

    lax.fori_loop(0, coarse.shape[0], scatter, 0)


def deliver_kernel(n_gy, n_gz, outgoing, received, send_sem, recv_sem, own_sem):
    gy, gz = lax.axis_index("gy"), lax.axis_index("gz")
    me = gy * n_gz + gz
    shifts = [
        (dy, dz) for dy in range(n_gy) for dz in range(n_gz) if dy + dz > 0
    ]
    shifts.sort(key=lambda shift: -min(shift[0], n_gy - shift[0]))
    barrier = pltpu.get_barrier_semaphore()
    targets = []
    for dy, dz in shifts:
        there = (lax.rem(gy + dy, n_gy), lax.rem(gz + dz, n_gz))
        targets.append(there)
        pl.semaphore_signal(
            barrier, inc=1, device_id={"gy": there[0], "gz": there[1]}, device_id_type=MESH
        )
    own = pltpu.make_async_copy(outgoing.at[me], received.at[me], own_sem)
    own.start()
    pl.semaphore_wait(barrier, len(shifts))
    copies = []
    for k, there in enumerate(targets):
        copy = pltpu.make_async_remote_copy(
            src_ref=outgoing.at[there[0] * n_gz + there[1]],
            dst_ref=received.at[me],
            send_sem=send_sem.at[k],
            recv_sem=recv_sem.at[k],
            device_id={"gy": there[0], "gz": there[1]},
            device_id_type=MESH,
        )
        copy.start()
        copies.append(copy)
    own.wait()
    for copy in copies:
        copy.wait()


def spread_kernel(sent, outgoing, received, lists, send_sem, recv_sem, own_sem):
    gy, gz = lax.axis_index("gy"), lax.axis_index("gz")
    half, place = gy // 2, lax.rem(gy, 2)
    me = gy * 2 + gz
    capacity = received.shape[1]

    def at(step):
        h, y, z = step
        there_half = 1 - half if h else half
        there_place = 1 - place if y else place
        return there_half * 2 + there_place, 1 - gz if z else gz

    steps = [(h, y, z) for h in (0, 1) for y in (0, 1) for z in (0, 1) if h + y + z]
    barrier = pltpu.get_barrier_semaphore()
    for step in steps:
        there = at(step)
        pl.semaphore_signal(
            barrier, inc=1, device_id={"gy": there[0], "gz": there[1]}, device_id_type=MESH
        )
    own = pltpu.make_async_copy(
        outgoing.at[pl.ds(me * capacity, capacity)], received.at[me], own_sem
    )
    own.start()
    pl.semaphore_wait(barrier, len(steps))

    def copy(k, step, source, target):
        there = at(step)
        return pltpu.make_async_remote_copy(
            src_ref=source, dst_ref=target, send_sem=send_sem.at[k], recv_sem=recv_sem.at[k],
            device_id={"gy": there[0], "gz": there[1]}, device_id_type=MESH,
        )

    def direct(step):
        there = at(step)
        count = capacity // 2 if step[0] else capacity
        return copy(
            steps.index(step), step,
            outgoing.at[pl.ds((there[0] * 2 + there[1]) * capacity, count)],
            received.at[me, pl.ds(0, count)],
        )

    mine, beside = place * 2 + gz, (1 - place) * 2 + gz
    rows = pl.ds(0, 1 + sent)
    tail = pl.ds(received.shape[0] * capacity, 1 + sent)
    across = copy(7, (1, 0, 0), outgoing.at[tail], lists.at[mine, rows])
    along = copy(8, (0, 1, 0), lists.at[mine, rows], lists.at[mine, rows])
    to_core = copy(9, (0, 0, 1), lists.at[mine, rows], lists.at[mine, rows])
    to_core_too = copy(10, (0, 0, 1), lists.at[beside, rows], lists.at[beside, rows])
    early = [direct((0, 1, 0)), direct((0, 0, 1))]
    late = [direct(step) for step in ((1, 0, 0), (1, 0, 1), (1, 1, 0), (1, 1, 1), (0, 1, 1))]
    across.start()
    for one in early:
        one.start()
    across.wait_recv()
    along.start()
    to_core.start()
    for one in late:
        one.start()
    along.wait_recv()
    to_core_too.start()
    own.wait()
    across.wait_send()
    along.wait_send()
    for one in early + late + [to_core, to_core_too]:
        one.wait()


def gather_kernel(sent, base, hbm_lists, received, lists, tiles, sems):
    direct = tiles.shape[1] // 2
    half = lax.axis_index("gy") // 2
    me = lax.axis_index("gy") * 2 + lax.axis_index("gz")
    rows = pl.ds(0, 1 + sent)
    near = [half * 4 + k for k in range(4)]
    far = [(1 - half) * 4 + k for k in range(4)]
    low = pl.ds(0, direct)
    whole = [
        pltpu.make_async_copy(base.at[near[k]], tiles.at[k], sems.at[0, k]) for k in range(4)
    ]
    listed = [
        pltpu.make_async_copy(hbm_lists.at[k, rows], lists.at[k, rows], sems.at[1, k])
        for k in range(4)
    ]
    part = [
        pltpu.make_async_copy(base.at[far[k], low], tiles.at[4 + k, low], sems.at[2, k])
        for k in range(4)
    ]
    stores = [
        pltpu.make_async_copy(tiles.at[k], received.at[(near + far)[k]], sems.at[3 + k // 4, k % 4])
        for k in range(8)
    ]
    for one in whole + listed + part:
        one.start()
    for k in range(4):
        whole[k].wait()
        stores[k].start()
    for k in range(4):
        listed[k].wait()
        part[k].wait()
        header = lists[k, 0, 0:1, :]
        lane = lax.broadcasted_iota(jnp.int32, header.shape, 1)
        start = jnp.sum(jnp.where((lane >= half * 4) & (lane < me), header, 0.0))
        count = jnp.sum(jnp.where(lane == me, header, 0.0)).astype(jnp.int32)
        later = lists[k, pl.ds(1 + start.astype(jnp.int32), direct)]
        slot = lax.broadcasted_iota(jnp.int32, later.shape, 0)
        tiles[4 + k, pl.ds(direct, direct)] = jnp.where(slot < count, later, 0.0)
        stores[4 + k].start()
    for one in stores:
        one.wait()


def spread(outgoing, group, room, levels, level):
    capacity = (outgoing.shape[0] - room - 1) // group
    tile = outgoing.shape[1:]
    def branch(number, sent):
        def run(outgoing):
            base, lists = pl.pallas_call(
                functools.partial(spread_kernel, sent),
                out_shape=[
                    jax.ShapeDtypeStruct((group, capacity) + tile, jnp.float32),
                    jax.ShapeDtypeStruct((group // 2, room + 1) + tile, jnp.float32),
                ],
                in_specs=[pl.BlockSpec(memory_space=pl.ANY)],
                out_specs=[pl.BlockSpec(memory_space=pl.ANY)] * 2,
                scratch_shapes=[
                    pltpu.SemaphoreType.DMA((11,)),
                    pltpu.SemaphoreType.DMA((11,)),
                    pltpu.SemaphoreType.DMA,
                ],
                compiler_params=pltpu.CompilerParams(
                    collective_id=2 + number, has_side_effects=True
                ),
                name="spread",
            )(outgoing)
            return pl.pallas_call(
                functools.partial(gather_kernel, sent),
                in_specs=[pl.BlockSpec(memory_space=pl.ANY)] * 2,
                out_specs=pl.BlockSpec(memory_space=pltpu.HBM),
                scratch_shapes=[
                    pltpu.VMEM((group // 2, room + 1) + tile, jnp.float32),
                    pltpu.VMEM((group, capacity) + tile, jnp.float32),
                    pltpu.SemaphoreType.DMA((5, group // 2)),
                ],
                out_shape=jax.ShapeDtypeStruct(base.shape, jnp.float32),
                compiler_params=pltpu.CompilerParams(vmem_limit_bytes=LIMIT),
                name="gather",
            )(base, lists)

        return run

    branches = [branch(k, sent) for k, sent in enumerate(levels + (room,))]
    return lax.switch(level, branches, outgoing)


def local(sizes, nodes, spacing_x, spacing_z, factor_x, gain_x, factor_z, gain_z, receivers):
    n_gx, n_gy, n_gz = sizes
    length, lines, depth = nodes.shape
    half, width = length // 2, depth // 2
    group = n_gy * n_gz
    blocks = half * lines // LINES
    capacity = max(2, blocks // group * 2)
    listed = n_gy == 4 and n_gz == 2
    direct = capacity // 2
    room = group // 2 * (capacity - direct) if listed else 0
    levels = tuple(room * k // 32 for k in (12, 16, 19))
    scalars, coefz, placed, header = pl.pallas_call(
        functools.partial(prepare_kernel, group=group, capacity=capacity, listed=listed),
        out_shape=[
            jax.ShapeDtypeStruct((32, 128), jnp.float32),
            jax.ShapeDtypeStruct((8, width), jnp.float32),
            jax.ShapeDtypeStruct((1, blocks), jnp.int32),
            jax.ShapeDtypeStruct((2 * LINES, 128), jnp.float32),
        ],
        compiler_params=pltpu.CompilerParams(vmem_limit_bytes=LIMIT),
        name="prepare",
    )(
        spacing_x.reshape(1, -1), spacing_z.reshape(1, -1), factor_x, gain_x.reshape(1, -1),
        receivers.reshape(1, -1),
    )
    gain_row = gain_z.reshape(1, width)
    vmem = pl.BlockSpec(memory_space=pltpu.VMEM)
    smem = pl.BlockSpec(memory_space=pltpu.SMEM)
    hbm = pl.BlockSpec(memory_space=pl.ANY)

    planes, most = pl.pallas_call(
        functools.partial(exchange_first, n_gx, n_gy),
        out_shape=[
            jax.ShapeDtypeStruct((3, lines, depth), jnp.float32),
            jax.ShapeDtypeStruct((8, 128), jnp.float32),
        ],
        in_specs=[smem, hbm],
        out_specs=[vmem, vmem],
        scratch_shapes=[
            pltpu.VMEM((length, lines, depth), jnp.float32),
            pltpu.VMEM((lines, depth), jnp.float32),
            pltpu.VMEM((lines, depth), jnp.float32),
            pltpu.VMEM((2, lines + 8, depth), jnp.float32),
            pltpu.VMEM((n_gx, lines + 8, depth), jnp.float32),
            pltpu.VMEM((n_gx, 8, 128), jnp.float32),
            pltpu.VMEM((n_gy, 8, 128), jnp.float32),
            pltpu.SemaphoreType.DMA((n_gx + 1,)),
            pltpu.SemaphoreType.DMA((n_gx + 1,)),
            pltpu.SemaphoreType.DMA((n_gx,)),
            pltpu.SemaphoreType.DMA((n_gx,)),
            pltpu.SemaphoreType.DMA((n_gy,)),
            pltpu.SemaphoreType.DMA((n_gy,)),
            pltpu.SemaphoreType.DMA((2,)),
        ],
        compiler_params=pltpu.CompilerParams(
            collective_id=0, has_side_effects=True, vmem_limit_bytes=LIMIT
        ),
        name="exchange_first",
    )(scalars, nodes)

    chunks = 4
    rows = lines // chunks
    params = pltpu.CompilerParams(
        dimension_semantics=("arbitrary",), vmem_limit_bytes=LIMIT
    )
    detail_x, coarse_x, payload = pl.pallas_call(
        functools.partial(first_kernel, count=n_gx),
        grid=(chunks,),
        in_specs=[
            pl.BlockSpec((length, rows, depth), lambda i: (0, i, 0)),
            pl.BlockSpec((3, rows, depth), lambda i: (0, i, 0)),
            pl.BlockSpec((8, 128), lambda i: (0, 0)),
            smem,
            pl.BlockSpec((8, width), lambda i: (0, 0)),
            pl.BlockSpec((width, width), lambda i: (0, 0)),
            pl.BlockSpec((1, width), lambda i: (0, 0)),
        ],
        out_specs=[
            pl.BlockSpec((half, rows, depth), lambda i: (0, i, 0)),
            pl.BlockSpec((half, rows, depth), lambda i: (0, i, 0)),
            pl.BlockSpec((1, 8, half * rows), lambda i: (i, 0, 0)),
        ],
        out_shape=[
            jax.ShapeDtypeStruct((half, lines, depth), jnp.float32),
            jax.ShapeDtypeStruct((half, lines, depth), jnp.float32),
            jax.ShapeDtypeStruct((chunks, 8, half * rows), jnp.float32),
        ],
        scratch_shapes=[pltpu.VMEM((8, depth), jnp.float32)],
        compiler_params=params,
        name="pass_first",
    )(nodes, planes, most, scalars, coefz, factor_z, gain_row)

    gathered = lax.all_gather(payload, "gz")

    held = group * capacity + (room + 1 if listed else 1)
    detail_z, outgoing, level = pl.pallas_call(
        functools.partial(
            third_kernel, count=n_gz, chunks=chunks, levels=levels, head=group * capacity
        ),
        grid=(chunks,),
        in_specs=[
            smem,
            pl.BlockSpec((half, rows, depth), lambda i: (0, i, 0)),
            pl.BlockSpec((n_gz, 1, 8, half * rows), lambda i: (0, i, 0, 0)),
            pl.BlockSpec((8, width), lambda i: (0, 0)),
            pl.BlockSpec((width, width), lambda i: (0, 0)),
            pl.BlockSpec((1, width), lambda i: (0, 0)),
            pl.BlockSpec((2 * LINES, width), lambda i: (0, 0)),
        ],
        out_specs=[
            pl.BlockSpec((half, rows, width), lambda i: (0, i, 0)),
            pl.BlockSpec((held, 2 * LINES, width), lambda i: (0, 0, 0)),
            smem,
        ],
        out_shape=[
            jax.ShapeDtypeStruct((half, lines, width), jnp.float32),
            jax.ShapeDtypeStruct((held, 2 * LINES, width), jnp.float32),
            jax.ShapeDtypeStruct((1,), jnp.int32),
        ],
        scratch_shapes=[
            pltpu.VMEM((depth, depth), jnp.float32),
            pltpu.VMEM((8, depth), jnp.float32),
            pltpu.VMEM((2, half * rows // 8, 8, width), jnp.float32),
        ],
        compiler_params=params,
        name="pass_third",
    )(placed, coarse_x, gathered, coefz, factor_z, gain_row, header)

    if listed:
        received = spread(outgoing, group, room, levels, level[0])
    else:
        outgoing = outgoing[: group * capacity].reshape(group, capacity, 2 * LINES, width)
        received = pl.pallas_call(
            functools.partial(deliver_kernel, n_gy, n_gz),
            out_shape=jax.ShapeDtypeStruct(outgoing.shape, jnp.float32),
            in_specs=[hbm],
            out_specs=hbm,
            scratch_shapes=[
                pltpu.SemaphoreType.DMA((group - 1,)),
                pltpu.SemaphoreType.DMA((group - 1,)),
                pltpu.SemaphoreType.DMA,
            ],
            compiler_params=pltpu.CompilerParams(collective_id=1, has_side_effects=True),
            name="deliver",
        )(outgoing)
    return (
        detail_x,
        detail_z,
        received.reshape(1, group, capacity, 2, LINES, width),
    )


def solution(mesh):
    sizes = tuple(mesh.shape[axis] for axis in ("gx", "gy", "gz"))
    return jax.shard_map(
        functools.partial(local, sizes),
        mesh=mesh,
        in_specs=(
            P("gx", "gy", "gz"),
            P(),
            P(),
            P("gx", None),
            P("gx"),
            P("gz", None),
            P("gz"),
            P(("gx", "gy", "gz"), None),
        ),
        out_specs=(
            P("gx", "gy", "gz"),
            P("gx", "gy", "gz"),
            P(("gx", "gy", "gz"), None, None, None, None, None),
        ),
        check_vma=False,
    )
```
